128 devices in a mesh: depth: 16 (over y, x), cross: 8 (over z, core).
Axes of the slice: x: 4, y: 4, z: 4, core: 2. Of those that a mesh axis runs over, the one named last changes fastest.
Arguments:
- flame_heat_values: bfloat16 [256, 1024, 2048], P('depth', 'cross'), may hold values from -6 to 6
- lookup_entry_index: int32 [256, 1024, 2048], P('depth', 'cross'), may hold values from 0 to 15
- transfer_lookup_table: float32 [4, 16], replicated, may hold values from 0.1 to 1
Outputs:
- picture: float32 [4, 1024, 2048], P(None, 'cross', 'depth')
The draws below stay inside these ranges and needn't reach their ends.
All inputs are finite; a program needn't handle non-finite values.
Results may differ from the reference program's by a relative error of at most 0.0003.
Values may be sent and summed in bfloat16 or wider, within the bound.
No kernel may reach another device: no remote copies, remote signals or barrier semaphores. Data moves between devices by JAX's collectives and lax.ppermute only.
A program may use at most 320 MiB of HBM per device.

```python
import jax
import jax.numpy as jnp
from jax import lax

FRAME_BREADTH = 2048
M = 16
SIGHT_SAMPLES = 256
FRAME_TALLNESS = 1024


def touch_ends(result, rng, least, high):
    extent = result.shape
    index_at = [jax.random.randint(jax.random.fold_in(rng, axis), (), 0, extent[axis]) for axis in range(len(extent))]
    result = result.at[tuple(index_at)].set(least)
    longest = extent.index(max(extent))
    index_at[longest] = (index_at[longest] + 1) % extent[longest]
    return result.at[tuple(index_at)].set(high)


def shard_levels(key, shape, shards, low, high):
    factor_of, own = 1.0, jax.random.fold_in(key, 6)
    for position, shards_of in shards:
        heights = jnp.exp(jax.random.uniform(jax.random.fold_in(own, position), (shards_of,), jnp.float32, low / len(shards), high / len(shards)))
        factor_of = factor_of * jnp.repeat(heights, shape[position] // shards_of).reshape([-1 if axis == position else 1 for axis in range(len(shape))])
    return factor_of


def scatter_about(key, dims, spread, most, split=(), held_as=jnp.bfloat16):
    gain = shard_levels(key, dims, split, -0.22, 0.18) if split else 1.0
    array = jax.random.normal(key, dims, jnp.float32) * spread * gain
    return jnp.minimum(jnp.maximum(array, -most), most).astype(held_as)


def setup_inputs(seed: int = 0) -> dict:
    seeds = jax.random.split(jax.random.key(seed), 4)
    flame_heat_values = scatter_about(seeds[0], (SIGHT_SAMPLES, FRAME_TALLNESS, FRAME_BREADTH), 1.0, 6.0, ((0, 16), (1, 8)))
    lookup_entry_index = touch_ends(jax.random.randint(seeds[1], (SIGHT_SAMPLES, FRAME_TALLNESS, FRAME_BREADTH), 0, M), jax.random.fold_in(seeds[1], 1), 0, M - 1).astype(jnp.int32)
    transfer_lookup_table = jnp.clip(jax.random.uniform(seeds[2], (4, M), jnp.float32, 0.1, 1.0), 0.1, 1.0)
    return dict(flame_heat_values=flame_heat_values, lookup_entry_index=lookup_entry_index, transfer_lookup_table=transfer_lookup_table)


def reference(flame_heat_values, lookup_entry_index, transfer_lookup_table):
    haloed_heat_mesh = jnp.pad(flame_heat_values, 1)
    light_depth = 1.0 / 3.0
    light_row = 2.0 / 3.0
    light_col = 2.0 / 3.0
    scale_alpha = 4.0 / SIGHT_SAMPLES

    def advance(carry, position_number):
        colors, trans = carry
        heat_section = lax.dynamic_slice_in_dim(haloed_heat_mesh, position_number, 3, 0).astype(jnp.float32)
        centre = heat_section[1, 1:-1, 1:-1]
        grad_depth = 0.5 * (heat_section[2, 1:-1, 1:-1] - heat_section[0, 1:-1, 1:-1])
        grad_row = 0.5 * (heat_section[1, 2:, 1:-1] - heat_section[1, :-2, 1:-1])
        grad_col = 0.5 * (heat_section[1, 1:-1, 2:] - heat_section[1, 1:-1, :-2])
        lit = grad_depth * light_depth + grad_row * light_row + grad_col * light_col
        square = grad_depth * grad_depth + grad_row * grad_row + grad_col * grad_col
        shade = 0.3 + 0.7 * lit * lit / (square + 1.0)
        entry = lax.dynamic_index_in_dim(lookup_entry_index, position_number, 0, keepdims=False)
        looked = jnp.take(transfer_lookup_table, entry, axis=1)
        alpha = scale_alpha * looked[3] * jax.nn.sigmoid(2.0 * centre)
        colors = colors + looked[:3] * (shade * alpha * trans)[None]
        trans = trans * (1.0 - alpha)
        return (colors, trans), None

    start = (jnp.zeros((3, FRAME_TALLNESS, FRAME_BREADTH), jnp.float32), jnp.ones((FRAME_TALLNESS, FRAME_BREADTH), jnp.float32))
    (colors, trans), unused = lax.scan(advance, start, jnp.arange(SIGHT_SAMPLES, dtype=jnp.int32))
    return jnp.concatenate([colors, (1.0 - trans)[None]], axis=0)
```

```python
import functools

import jax
import jax.numpy as jnp
import numpy as np
from jax import lax
from jax.experimental import pallas as pl
from jax.experimental.pallas import tpu as pltpu
from jax.sharding import PartitionSpec as P

LANES = 128
SUBLANES = 8
PARTS = 2
UNITS = 4
WIDTH = 1024
PIECES = 16
f32 = jnp.float32
LANE_LOOKUP = lax.GatherDimensionNumbers(
    offset_dims=(),
    collapsed_slice_dims=(1,),
    start_index_map=(1,),
    operand_batching_dims=(0,),
    start_indices_batching_dims=(0,),
)
KAPPA = -2.0 / float(np.log(2.0))
HIGH_STEPS = 32766.0
LOW_STEPS = 65535.0
CENTRE = 16.0
STEPS = 2340.0
LEAST = 2.0**-29.9


def brick_kernel(table_ref, diff_ref, left_ref, heat_ref, right_ref, above_ref, below_ref, before_ref, after_ref, upper_ref,
                 lower_ref, entry_ref, out_ref, t, dv, *, block, blocks, sight):
    layers, rows, width = heat_ref.shape
    strips = width // LANES
    j = pl.program_id(0)
    opaque = LOW_STEPS * sight / 4.0
    bias = float(np.log2(opaque))

    def kept(value):
        return value.astype(f32) * KAPPA + bias

    for s in range(strips):
        cols = slice(s * LANES, (s + 1) * LANES)

        def convert(z, carry):
            t[z + 1, s, 0:8, :] = kept(above_ref[z, 8:16, cols])
            t[z + 1, s, 8 : 8 + rows, :] = kept(heat_ref[z, :, cols])
            t[z + 1, s, 8 + rows : 16 + rows, :] = kept(below_ref[z, 0:8, cols])
            return carry

        lax.fori_loop(0, layers, convert, 0, unroll=4)
        t[0, s, 8 : 8 + rows, :] = kept(before_ref[:, cols])
        t[layers + 1, s, 8 : 8 + rows, :] = kept(after_ref[:, cols])
        if block == 0:
            up = kept(upper_ref[:, cols])
            for z in range(layers):
                t[z + 1, s, 7:8, :] = up[z : z + 1]
        if block == blocks - 1:
            low = kept(lower_ref[:, cols])
            for z in range(layers):
                t[z + 1, s, 8 + rows : 9 + rows, :] = low[z : z + 1]

    zero = jnp.zeros((), jnp.bfloat16)
    left = jnp.where(j == 0, zero, left_ref[...])
    right = jnp.where(j == pl.num_programs(0) - 1, zero, right_ref[...])
    pieces = [left] + [heat_ref[:, :, s * LANES : (s + 1) * LANES] for s in range(strips)] + [right]
    for s in range(0, strips, 2):
        window = jnp.concatenate(pieces[s : s + 4], axis=2).reshape(layers * rows, 4 * LANES)
        moved = jnp.dot(window, diff_ref[...], preferred_element_type=f32).reshape(layers, rows, 2 * LANES)
        dv[:, s] = moved[:, :, :LANES] * KAPPA
        dv[:, s + 1] = moved[:, :, LANES:] * KAPPA

    tables = [jnp.broadcast_to(table_ref[pair : pair + 1, :], (SUBLANES, LANES)) for pair in range(2)]

    def looked(entry):
        rg, ba = [
            lax.gather(table, entry[:, :, None], LANE_LOOKUP, (1, 1), mode=lax.GatherScatterMode.PROMISE_IN_BOUNDS)
            for table in tables
        ]
        return rg.astype(f32), (rg & 0xFFFF).astype(f32), ba.astype(f32), (ba & 0xFFFF).astype(f32)

    scale = 0.7 / 9.0
    scales = [scale / (HIGH_STEPS * 65536.0), scale / LOW_STEPS, scale / (HIGH_STEPS * 65536.0)]
    groups = rows // (SUBLANES * UNITS)

    def body(g, carry):
        s = g // groups
        cols = pl.ds(pl.multiple_of(s * LANES, LANES), LANES)
        units = []
        for u in range(UNITS):
            r0 = pl.multiple_of((g % groups) * (SUBLANES * UNITS) + u * SUBLANES, SUBLANES)
            units.append(
                dict(
                    r0=r0,
                    trans=jnp.ones((SUBLANES, LANES), f32),
                    colors=[jnp.zeros((SUBLANES, LANES), f32) for channel in range(3)],
                    prev=t[0, s, pl.ds(8 + r0, 8), :],
                    cur=t[1, s, pl.ds(8 + r0, 8), :],
                )
            )
        for z in range(layers):
            for unit in units:
                r0 = unit["r0"]
                nxt = t[z + 2, s, pl.ds(8 + r0, 8), :]
                a = nxt - unit["prev"]
                b = t[z + 1, s, pl.ds(9 + r0, 8), :] - t[z + 1, s, pl.ds(7 + r0, 8), :]
                c = dv[z, s, pl.ds(r0, 8), :]
                m = b + c
                lit = a + m + m
                square = (a * a + b * b) + (c * c + 4.0 * KAPPA * KAPPA)
                shade = lit * lit * pl.reciprocal(square, approx=True) + 0.3 / scale
                red, green, blue, weight = looked(entry_ref[z, pl.ds(r0, 8), cols])
                alpha = weight * pl.reciprocal(jnp.exp2(unit["cur"]) + opaque, approx=True)
                part = alpha * unit["trans"]
                unit["trans"] = unit["trans"] - part
                shown = shade * part
                unit["colors"] = [old + new * shown for old, new in zip(unit["colors"], (red, green, blue))]
                unit["prev"], unit["cur"] = unit["cur"], nxt
        for pair in range(0, UNITS, 2):
            both = units[pair : pair + 2]
            for channel in range(4):
                value = jnp.concatenate(
                    [unit["colors"][channel] * scales[channel] if channel < 3 else 1.0 - unit["trans"] for unit in both], axis=0
                )
                code = jnp.round((jnp.log2(jnp.maximum(value, LEAST)) + CENTRE) * STEPS)
                out_ref[s, channel, pl.ds(pl.multiple_of(both[0]["r0"], 16), 16), :] = code.astype(jnp.int32).astype(jnp.int16)
        return carry

    lax.fori_loop(0, strips * groups, body, 0)


def brick(table, diff, heat, before, after, upper, lower, entry, block, sight):
    layers, all_rows, columns = heat.shape
    rows = all_rows // PARTS
    n = columns // WIDTH
    per = WIDTH // LANES
    col_blocks = columns // LANES
    sub = rows // 16
    return pl.pallas_call(
        functools.partial(brick_kernel, block=block, blocks=PARTS, sight=sight),
        grid=(n,),
        in_specs=[
            pl.BlockSpec((2, LANES), lambda j: (0, 0)),
            pl.BlockSpec((4 * LANES, 2 * LANES), lambda j: (0, 0)),
            pl.BlockSpec((layers, rows, LANES), lambda j: (0, block, jnp.maximum(j * per - 1, 0))),
            pl.BlockSpec((layers, rows, WIDTH), lambda j: (0, block, j)),
            pl.BlockSpec((layers, rows, LANES), lambda j: (0, block, jnp.minimum(j * per + per, col_blocks - 1))),
            pl.BlockSpec((layers, 16, WIDTH), lambda j: (0, max(sub * block - 1, 0), j)),
            pl.BlockSpec((layers, 16, WIDTH), lambda j: (0, min(sub * block + sub, all_rows // 16 - 1), j)),
            pl.BlockSpec((rows, WIDTH), lambda j: (block, j)),
            pl.BlockSpec((rows, WIDTH), lambda j: (block, j)),
            pl.BlockSpec((layers, WIDTH), lambda j: (0, j)),
            pl.BlockSpec((layers, WIDTH), lambda j: (0, j)),
            pl.BlockSpec((layers, rows, WIDTH), lambda j: (0, block, j)),
        ],
        out_specs=pl.BlockSpec((per, 4, rows, LANES), lambda j: (j, 0, 0, 0)),
        out_shape=jax.ShapeDtypeStruct((col_blocks, 4, rows, LANES), jnp.int16),
        scratch_shapes=[
            pltpu.VMEM((layers + 2, per, rows + 16, LANES), f32),
            pltpu.VMEM((layers, per, rows, LANES), f32),
        ],
        compiler_params=pltpu.CompilerParams(vmem_limit_bytes=56 * 1024 * 1024),
        name="brick",
    )(table, diff, heat, heat, heat, heat, heat, before, after, upper, lower, entry)


def merge_kernel(got_ref, *rest):
    out_ref = rest[-1]
    count, channels, rows, lanes = got_ref.shape

    def body(g, carry):
        here = pl.ds(pl.multiple_of(g * 16, 16), 16)
        colors = [jnp.zeros((16, lanes), f32) for channel in range(3)]
        trans = jnp.ones((16, lanes), f32)
        for source in range(count):
            value = [
                jnp.exp2(got_ref[source, channel, here, :].astype(f32) * (1.0 / STEPS) - CENTRE) for channel in range(4)
            ]
            colors = [old + trans * new for old, new in zip(colors, value)]
            trans = trans - trans * value[3]
        for channel in range(4):
            out_ref[channel, here, :] = colors[channel] if channel < 3 else 1.0 - trans
        return carry

    lax.fori_loop(0, rows // 16, body, 0)


def merge(got, block, image):
    count, channels, rows, lanes = got.shape
    here = pl.BlockSpec((channels, rows, lanes), lambda i: (0, block, 0))
    operands, specs, aliases = [got], [pl.BlockSpec(got.shape, lambda i: (0, 0, 0, 0))], {}
    if image is not None:
        operands.append(image)
        specs.append(pl.BlockSpec(memory_space=pl.ANY))
        aliases = {1: 0}
    return pl.pallas_call(
        merge_kernel,
        grid=(1,),
        in_specs=specs,
        out_specs=here,
        out_shape=jax.ShapeDtypeStruct((channels, rows * PARTS, lanes), f32),
        input_output_aliases=aliases,
        name="merge",
    )(*operands)


def difference_matrix():
    m = np.zeros((4 * LANES, 2 * LANES), np.float32)
    n = np.arange(2 * LANES)
    m[LANES + n + 1, n] = 1
    m[LANES + n - 1, n] = -1
    return jnp.asarray(m, jnp.bfloat16)


def packed(table):
    low = jnp.round(table[1::2] * LOW_STEPS)
    high = jnp.round(table[0::2] * HIGH_STEPS - low * (1.0 / 65536.0))
    words = high.astype(jnp.int32) * 65536 + low.astype(jnp.int32)
    return jnp.pad(words, ((0, 0), (0, LANES - table.shape[1])))


def local(heat, entry, table):
    count = lax.axis_size("depth")
    sides = lax.axis_size("cross")
    sight = heat.shape[0] * count
    on, back = [(i, i + 1) for i in range(count - 1)], [(i + 1, i) for i in range(count - 1)]
    down, up = [(i, i + 1) for i in range(sides - 1)], [(i + 1, i) for i in range(sides - 1)]
    upper = lax.ppermute(heat[:, -1, :], "cross", down)
    lower = lax.ppermute(heat[:, 0, :], "cross", up)
    before = lax.ppermute(heat[-1], "depth", on)
    after = lax.ppermute(heat[0], "depth", back)
    words, diff = packed(table), difference_matrix()
    image = None
    sent = []
    for block in range(PARTS):
        codes = brick(words, diff, heat, before, after, upper, lower, entry, block, sight)
        sent.append(lax.all_to_all(codes, "depth", 0, 0, tiled=True))
    for block in range(PARTS):
        image = merge(sent[block], block, image)
    return image


def solution(mesh):
    in_specs = (P("depth", "cross", None), P("depth", "cross", None), P())
    out_specs = P(None, "cross", "depth")
    return jax.shard_map(local, mesh=mesh, in_specs=in_specs, out_specs=out_specs, check_vma=False)
```

```python
import jax
import jax.numpy as jnp
import numpy as np
from jax import lax
from jax.experimental import pallas as pl
from jax.experimental.pallas import tpu as pltpu
from jax.sharding import PartitionSpec as P

LANES = 128
SUBLANES = 8
PIECE = 256
f32 = jnp.float32
LANE_LOOKUP = lax.GatherDimensionNumbers(
    offset_dims=(),
    collapsed_slice_dims=(1,),
    start_index_map=(1,),
    operand_batching_dims=(0,),
    start_indices_batching_dims=(0,),
)
KAPPA = -2.0 / float(np.log(2.0))
HIGH_STEPS = 32766.0
LOW_STEPS = 65535.0
CENTRE = 16.0
STEPS = 2340.0
LEAST = 2.0**-29.9


def strip_pipeline(table_ref, rims_ref, before_ref, after_ref, heat_hbm, entry_hbm, state_ref, out_ref, diff, heat, entry,
                   rim_rows, ta, da, tb, db, heat_sem, entry_sem, *, segments, mode, sight):
    all_rows, columns = heat_hbm.shape[1:]
    layers = heat_hbm.shape[0]
    height = segments[0][1]
    count = columns // PIECE
    strips = PIECE // LANES
    if mode == "all":
        centres, shift, extras = list(range(1, layers + 1)), 1, {0: "before", layers + 1: "after"}
    elif mode == "mid":
        centres, shift, extras = list(range(1, layers - 1)), 0, {0: 0, layers - 1: layers - 1}
    else:
        centres, shift, extras = [1, 4], 1, {0: "before", 2: 1, 3: 2, 5: "after"}
    stride = centres[1] - centres[0]
    parts = strips if height > 16 else 1
    share = len(centres) // parts
    batch = min(share, 128 // height)
    while share % batch:
        batch -= 1
    units_at_once = 4 if height % 32 == 0 else 2

    def heat_copies(p):
        cols = pl.ds(pl.multiple_of(p * PIECE, PIECE), PIECE)
        into = pl.ds(pl.multiple_of(2 * LANES + p * PIECE, LANES), PIECE)
        found = []
        for k, (row, _) in enumerate(segments):
            low, high = max(row - 16, 0), min(row + height + 16, all_rows)
            target = pl.ds(16 - (row - low), high - low)
            if mode == "ends":
                pairs = [(0, 0, 2), (layers - 2, 2, 2)]
            else:
                pairs = [(0, 0, layers)]
            for n, (source, first, size) in enumerate(pairs):
                found.append(
                    pltpu.make_async_copy(
                        heat_hbm.at[pl.ds(source, size), pl.ds(low, high - low), cols],
                        heat.at[k, pl.ds(first, size), target, into],
                        heat_sem.at[2 * k + n, p],
                    )
                )
        return found

    def entry_copies(p):
        cols = pl.ds(pl.multiple_of(p * PIECE, PIECE), PIECE)
        found = []
        for k, (row, _) in enumerate(segments):
            if mode == "ends":
                pairs = [(0, 0, 1), (layers - 1, 1, 1)]
            else:
                pairs = [(1 if mode == "mid" else 0, 0, len(centres))]
            for n, (source, first, size) in enumerate(pairs):
                found.append(
                    pltpu.make_async_copy(
                        entry_hbm.at[pl.ds(source, size), pl.ds(row, height), cols],
                        entry.at[pl.ds(first, size), pl.ds(k * height, height), cols],
                        entry_sem.at[2 * k + n, p],
                    )
                )
        return found

    def start(copies):
        for copy in copies:
            copy.start()

    def wait(copies):
        for copy in copies:
            copy.wait()

    start(heat_copies(0))
    start(heat_copies(1))
    for p in range(count):
        start(entry_copies(p))
        if p + 2 < count:
            start(heat_copies(p + 2))

    heat[:, :, :, 0 : 2 * LANES] = jnp.zeros(heat.shape[:3] + (2 * LANES,), jnp.bfloat16)
    heat[:, :, :, 2 * LANES + columns :] = jnp.zeros(heat.shape[:3] + (LANES,), jnp.bfloat16)
    k = lax.broadcasted_iota(jnp.int32, diff.shape, 0) - lax.broadcasted_iota(jnp.int32, diff.shape, 1)
    diff[...] = jnp.where(k == LANES + 1, 1.0, jnp.where(k == LANES - 1, -1.0, 0.0)).astype(jnp.bfloat16)
    if rims_ref is not None:
        rim_rows[...] = rims_ref[...].astype(f32)

    def prepare(p, seg, t, dv, n, qs):
        row = segments[seg][0]
        own = pl.ds(pl.multiple_of(p * PIECE, PIECE), PIECE)
        cols = pl.ds(pl.multiple_of(2 * LANES + p * PIECE, LANES), PIECE)
        wide = pl.ds(pl.multiple_of(LANES + p * PIECE, LANES), PIECE + 2 * LANES)
        mid = slice(16, 16 + height)

        def put(slot, first, value):
            for q in range(strips):
                t[q, slot, first : first + value.shape[0], :] = value[:, q * LANES : (q + 1) * LANES]

        for q in qs:
            for slot, source in extras.items():
                here = pl.multiple_of(p * PIECE + q * LANES, LANES)
                if source == "before":
                    value = before_ref[row : row + height, pl.ds(here, LANES)]
                elif source == "after":
                    value = after_ref[row : row + height, pl.ds(here, LANES)]
                else:
                    value = heat[seg, source, mid, pl.ds(2 * LANES + here, LANES)]
                t[q, slot, 8 : 8 + height, :] = value.astype(f32)
        for first in range(0, share, batch):
            at = n * share + first
            slot0 = centres[0] + stride * at
            if stride == 1:
                window = heat[seg, pl.ds(slot0 - shift, batch), mid, wide].reshape(batch * height, PIECE + 2 * LANES)
            else:
                window = jnp.concatenate([heat[seg, centres[0] - shift + stride * (at + m), mid, wide] for m in range(batch)], axis=0)
            moved = jnp.dot(window, diff[...], preferred_element_type=f32).reshape(batch, height, PIECE)
            for q in range(strips):
                dv[q, pl.ds(at, batch)] = moved[:, :, q * LANES : (q + 1) * LANES]
            for m in range(batch):
                slot = slot0 + stride * m
                z = slot - shift
                layer = z if mode != "ends" else jnp.where(at + m == 0, 0, layers - 1)
                put(slot, 8, heat[seg, z, mid, cols].astype(f32))
                if row == 0:
                    put(slot, 7, rim_rows[0, pl.ds(layer, 1), own])
                else:
                    put(slot, 0, heat[seg, z, 0:16, cols].astype(f32)[8:16])
                if row + height == all_rows:
                    put(slot, 8 + height, rim_rows[1, pl.ds(layer, 1), own])
                else:
                    put(slot, 8 + height, heat[seg, z, 16 + height : 32 + height, cols].astype(f32)[0:8])
                yield

    tables = []
    for pair in range(2):
        low_half = jnp.round(table_ref[2 * pair + 1 : 2 * pair + 2, :] * LOW_STEPS)
        high_half = jnp.round(table_ref[2 * pair : 2 * pair + 1, :] * HIGH_STEPS - low_half * (1.0 / 65536.0))
        words = high_half.astype(jnp.int32) * 65536 + low_half.astype(jnp.int32)
        tables.append(jnp.broadcast_to(words, (SUBLANES, LANES)))

    def looked(index):
        rg, ba = [
            lax.gather(table, index[:, :, None], LANE_LOOKUP, (1, 1), mode=lax.GatherScatterMode.PROMISE_IN_BOUNDS)
            for table in tables
        ]
        return rg.astype(f32), (rg & 0xFFFF).astype(f32), ba.astype(f32), (ba & 0xFFFF).astype(f32) * (4.0 / (sight * LOW_STEPS))

    scale = 0.7 / 9.0
    scales = [scale / (HIGH_STEPS * 65536.0), scale / LOW_STEPS, scale / (HIGH_STEPS * 65536.0)]

    def composite(p, seg, t, dv, qs):
        jobs = [(q, r0) for q in qs for r0 in range(0, height, SUBLANES)]
        size = units_at_once if parts > 1 else len(jobs)
        for group in range(0, len(jobs), size):
            units = []
            for q, r0 in jobs[group : group + size]:
                s = strips * p + q
                units.append(
                    dict(
                        q=q,
                        s=s,
                        r0=r0,
                        cols=pl.ds(pl.multiple_of(s * LANES, LANES), LANES),
                        trans=jnp.ones((SUBLANES, LANES), f32),
                        colors=[jnp.zeros((SUBLANES, LANES), f32) for channel in range(3)],
                        prev=t[q, centres[0] - 1, 8 + r0 : 16 + r0, :],
                        cur=t[q, centres[0], 8 + r0 : 16 + r0, :],
                    )
                )
            for at, slot in enumerate(centres):
                for unit in units:
                    q, r0 = unit["q"], unit["r0"]
                    if mode == "ends" and at == 1:
                        kept = [state_ref[unit["s"], channel, seg * height + r0 : seg * height + r0 + 8, :] for channel in range(4)]
                        unit["colors"] = [old + unit["trans"] * new for old, new in zip(unit["colors"], kept)]
                        unit["trans"] = unit["trans"] * kept[3]
                        unit["prev"], unit["cur"] = t[q, slot - 1, 8 + r0 : 16 + r0, :], t[q, slot, 8 + r0 : 16 + r0, :]
                    nxt = t[q, slot + 1, 8 + r0 : 16 + r0, :]
                    a = nxt - unit["prev"]
                    b = t[q, slot, 9 + r0 : 17 + r0, :] - t[q, slot, 7 + r0 : 15 + r0, :]
                    c = dv[q, at, r0 : r0 + 8, :]
                    m = b + c
                    lit = a + m + m
                    square = (a * a + b * b) + (c * c + 4.0)
                    shade = lit * lit * pl.reciprocal(square, approx=True) + 0.3 / scale
                    red, green, blue, weight = looked(entry[at, seg * height + r0 : seg * height + r0 + 8, unit["cols"]])
                    alpha = weight * pl.reciprocal(jnp.exp2(unit["cur"] * KAPPA) + 1.0, approx=True)
                    part = alpha * unit["trans"]
                    unit["trans"] = unit["trans"] - part
                    shown = shade * part
                    unit["colors"] = [old + new * shown for old, new in zip(unit["colors"], (red, green, blue))]
                    unit["prev"], unit["cur"] = unit["cur"], nxt
                yield
            for pair in range(0, len(units), 2):
                twin = units[pair : pair + 2]
                r0 = seg * height + twin[0]["r0"]
                for channel in range(4):
                    if mode == "mid":
                        values = [unit["colors"][channel] if channel < 3 else unit["trans"] for unit in twin]
                        out_ref[twin[0]["s"], channel, r0 : r0 + 16, :] = jnp.concatenate(values, axis=0)
                        continue
                    values = [unit["colors"][channel] * scales[channel] if channel < 3 else 1.0 - unit["trans"] for unit in twin]
                    code = jnp.round((jnp.log2(jnp.maximum(jnp.concatenate(values, axis=0), LEAST)) + CENTRE) * STEPS)
                    out_ref[twin[0]["s"], channel, r0 : r0 + 16, :] = code.astype(jnp.int32).astype(jnp.int16)

    def both(first, second):
        def part(n, carry):
            qs = [n] if parts > 1 else list(range(strips))
            following = prepare(*second, n, qs)
            groups = max(height // (SUBLANES * units_at_once), 1) if parts > 1 else 1
            steps = max(groups * len(centres) // share, 1)
            for at, step in enumerate(composite(*first, qs)):
                if at % steps == 0:
                    next(following, None)
            for step in following:
                pass
            return carry

        if parts > 1:
            lax.fori_loop(0, parts, part, 0)
        else:
            part(0, 0)

    wait(heat_copies(0))
    wait(heat_copies(1))
    for n in range(parts):
        for step in prepare(0, 0, ta, da, n, [n] if parts > 1 else list(range(strips))):
            pass

    def body(i, carry):
        @pl.when(i + 2 < count)
        def _():
            wait(heat_copies(i + 2))

        wait(entry_copies(i))
        both((i, 0, ta, da), (i, 1, tb, db))
        both((i, 1, tb, db), (jnp.minimum(i + 1, count - 1), 0, ta, da))
        return carry

    lax.fori_loop(0, count, body, 0)


def brick(table, heat, entry, segments, mode, sight, before=None, after=None, rims=None, state=None, codes=None, out_rows=None):
    layers, all_rows, columns = heat.shape
    height = segments[0][1]
    own_rows = 2 * height
    out_rows = out_rows or own_rows
    blocks = columns // LANES
    whole = pl.BlockSpec(memory_space=pl.ANY)
    given = {"table": (table, pl.BlockSpec((4, LANES), lambda i: (0, 0))), "heat": (heat, whole), "entry": (entry, whole)}
    if rims is not None:
        given["rims"] = (rims, pl.BlockSpec(rims.shape, lambda i: (0, 0, 0)))
    if before is not None:
        given["before"] = (before, pl.BlockSpec(before.shape, lambda i: (0, 0)))
        given["after"] = (after, pl.BlockSpec(after.shape, lambda i: (0, 0)))
    if state is not None:
        given["state"] = (state, pl.BlockSpec(state.shape, lambda i: (0, 0, 0, 0)))
    if codes is not None:
        given["codes"] = (codes, whole)
    names = list(given)
    held, centres = {"all": (layers, layers), "mid": (layers, layers - 2), "ends": (4, 2)}[mode]
    slots = {"all": layers + 2, "mid": layers, "ends": 6}[mode]
    t = pltpu.VMEM((PIECE // LANES, slots, height + 16, LANES), f32)
    dv = pltpu.VMEM((PIECE // LANES, centres, height, LANES), f32)

    def kernel(*refs):
        ref = dict(zip(names, refs))
        rest = refs[len(names) :]
        strip_pipeline(ref["table"], ref.get("rims"), ref.get("before"), ref.get("after"), ref["heat"], ref["entry"],
                       ref.get("state"), *rest, segments=segments, mode=mode, sight=sight)

    return pl.pallas_call(
        kernel,
        grid=(1,),
        in_specs=[given[name][1] for name in names],
        out_specs=pl.BlockSpec((blocks, 4, own_rows, LANES), lambda i: (0, 0, 0 if codes is None else 1, 0)),
        out_shape=jax.ShapeDtypeStruct((blocks, 4, out_rows, LANES), f32 if mode == "mid" else jnp.int16),
        scratch_shapes=[
            pltpu.VMEM((PIECE + 2 * LANES, PIECE), jnp.bfloat16),
            pltpu.VMEM((2, held, height + 32, columns + 3 * LANES), jnp.bfloat16),
            pltpu.VMEM((centres, own_rows, columns), jnp.int32),
            pltpu.VMEM((2, layers, columns), f32),
            t,
            dv,
            t,
            dv,
            pltpu.SemaphoreType.DMA((4, columns // PIECE)),
            pltpu.SemaphoreType.DMA((4, columns // PIECE)),
        ],
        input_output_aliases={} if codes is None else {names.index("codes"): 0},
        compiler_params=pltpu.CompilerParams(vmem_limit_bytes=44 * 1024 * 1024),
        name=mode + "_layers",
    )(*[given[name][0] for name in names])


def merge_kernel(got_ref, *rest):
    out_ref = rest[-1]
    count, channels, rows, lanes = got_ref.shape
    colors = [jnp.zeros((rows, lanes), f32) for channel in range(3)]
    trans = jnp.ones((rows, lanes), f32)
    for source in range(count):
        value = [jnp.exp2(got_ref[source, channel].astype(f32) * (1.0 / STEPS) - CENTRE) for channel in range(4)]
        colors = [old + trans * new for old, new in zip(colors, value)]
        trans = trans - trans * value[3]
    for channel in range(4):
        out_ref[channel] = colors[channel] if channel < 3 else 1.0 - trans


def merge(got, image, all_rows, place):
    count, channels, rows, lanes = got.shape
    operands, specs, aliases = [got], [pl.BlockSpec((count, channels, 16, lanes), lambda i: (0, 0, i, 0))], {}
    if image is not None:
        operands.append(image)
        specs.append(pl.BlockSpec(memory_space=pl.ANY))
        aliases = {1: 0}
    return pl.pallas_call(
        merge_kernel,
        grid=(rows // 16,),
        in_specs=specs,
        out_specs=pl.BlockSpec((channels, 16, lanes), lambda i: (0, place(i), 0)),
        out_shape=jax.ShapeDtypeStruct((channels, all_rows, lanes), f32),
        input_output_aliases=aliases,
        name="merge",
    )(*operands)


def local(heat, entry, table):
    count = lax.axis_size("depth")
    sides = lax.axis_size("cross")
    layers, rows, columns = heat.shape
    sight = layers * count
    on, back = [(i, i + 1) for i in range(count - 1)], [(i + 1, i) for i in range(count - 1)]
    before = lax.ppermute(heat[-1], "depth", on)
    after = lax.ppermute(heat[0], "depth", back)
    mine = jnp.stack([heat[:, -1, :], heat[:, 0, :]])
    every = lax.all_gather(mine, "cross", axis=0)
    me = lax.axis_index("cross")
    upper = lax.dynamic_index_in_dim(every, jnp.maximum(me - 1, 0), 0, keepdims=False)[0]
    lower = lax.dynamic_index_in_dim(every, jnp.minimum(me + 1, sides - 1), 0, keepdims=False)[1]
    nothing = jnp.zeros((), heat.dtype)
    rims = jnp.stack([jnp.where(me > 0, upper, nothing), jnp.where(me < sides - 1, lower, nothing)])
    table = jnp.pad(table, ((0, 0), (0, LANES - table.shape[1])))

    centre, inner, outer = ((48, 16), (64, 16)), ((16, 32), (80, 32)), ((0, 16), (112, 16))
    state = brick(table, heat, entry, centre, "mid", sight)
    codes = brick(table, heat, entry, inner, "all", sight, before=before, after=after)
    first = lax.all_to_all(codes, "depth", 0, 0, tiled=True)
    codes = brick(table, heat, entry, outer, "all", sight, before=before, after=after, rims=rims, out_rows=64)
    codes = brick(table, heat, entry, centre, "ends", sight, before=before, after=after, state=state, codes=codes, out_rows=64)
    second = lax.all_to_all(codes, "depth", 0, 0, tiled=True)
    image = merge(first, None, rows, lambda i: i + 1 + 2 * (i // 2))
    return merge(second, image, rows, lambda i: jnp.where(i == 0, 0, jnp.where(i == 1, 7, i + 1)))


def solution(mesh):
    in_specs = (P("depth", "cross", None), P("depth", "cross", None), P())
    out_specs = P(None, "cross", "depth")
    return jax.shard_map(local, mesh=mesh, in_specs=in_specs, out_specs=out_specs, check_vma=False)
```

```python
import jax
import jax.numpy as jnp
import numpy as np
from jax import lax
from jax.experimental import pallas as pl
from jax.experimental.pallas import tpu as pltpu
from jax.sharding import PartitionSpec as P

LANES = 128
SUBLANES = 8
PIECE = 256
LOAD = 256
f32 = jnp.float32
LANE_LOOKUP = lax.GatherDimensionNumbers(
    offset_dims=(),
    collapsed_slice_dims=(1,),
    start_index_map=(1,),
    operand_batching_dims=(0,),
    start_indices_batching_dims=(0,),
)
KAPPA = -2.0 / float(np.log(2.0))
HIGH_STEPS = 32766.0
LOW_STEPS = 65535.0
CENTRE = 16.0
STEPS = 2340.0
LEAST = 2.0**-29.9


def strip_pipeline(tables, rim_rows, inside, before_ref, after_ref, heat_hbm, entry_hbm, state_ref, out_hbm, out_ref, out_row, diff, heat, entry,
                   ta, da, tb, db, heat_sem, entry_sem, out_sem, *, segments, mode, sight):
    all_rows, columns = heat_hbm.shape[1:]
    layers = heat_hbm.shape[0]
    height = segments[0][1]
    count = columns // PIECE
    strips = PIECE // LANES
    if mode == "all":
        centres, shift, extras = list(range(1, layers + 1)), 1, {0: "before", layers + 1: "after"}
    elif mode == "mid":
        centres, shift, extras = list(range(1, layers - 1)), 0, {0: 0, layers - 1: layers - 1}
    else:
        centres, shift, extras = [1, 4], 1, {0: "before", 2: 1, 3: 2, 5: "after"}
    stride = centres[1] - centres[0]
    parts = strips if height > 16 else 1
    share = len(centres) // parts
    batch = min(share, 128 // height)
    while share % batch:
        batch -= 1
    units_at_once = 4 if height % 32 == 0 else 2

    load = columns if mode == "ends" else LOAD
    loads, each = columns // load, load // PIECE
    ahead = 2 if each == 1 else 1
    adjacent = segments[1][0] == segments[0][0] + height
    blocks_of_rows = [(segments[0][0], 0, 2 * height)] if adjacent else [(row, k * height, height) for k, (row, _) in enumerate(segments)]

    def heat_copies(p):
        cols = pl.ds(pl.multiple_of(p * load, load), load)
        into = pl.ds(pl.multiple_of(2 * LANES + p * load, LANES), load)
        found = []
        for k, (row, _) in enumerate(segments):
            low, high = max(row - 16, 0), min(row + height + 16, all_rows)
            target = pl.ds(16 - (row - low), high - low)
            pairs = [(0, 0, 2), (layers - 2, 2, 2)] if mode == "ends" else [(0, 0, layers)]
            for n, (source, first, size) in enumerate(pairs):
                found.append(
                    pltpu.make_async_copy(
                        heat_hbm.at[pl.ds(source, size), pl.ds(low, high - low), cols],
                        heat.at[k, pl.ds(first, size), target, into],
                        heat_sem.at[2 * k + n, p],
                    )
                )
        return found

    def entry_copies(p):
        cols = pl.ds(pl.multiple_of(p * load, load), load)
        found = []
        for k, (row, own, size) in enumerate(blocks_of_rows):
            if mode == "ends":
                pairs = [(0, 0, 1), (layers - 1, 1, 1)]
            else:
                pairs = [(1 if mode == "mid" else 0, 0, len(centres))]
            for n, (source, first, deep) in enumerate(pairs):
                found.append(
                    pltpu.make_async_copy(
                        entry_hbm.at[pl.ds(source, deep), pl.ds(row, size), cols],
                        entry.at[pl.ds(first, deep), pl.ds(own, size), cols],
                        entry_sem.at[2 * k + n, p],
                    )
                )
        return found

    def out_copy(p):
        here = pl.ds(p * (load // LANES), load // LANES)
        rows = pl.ds(out_row, 2 * height)
        return pltpu.make_async_copy(out_ref.at[here, :, rows], out_hbm.at[here, :, rows], out_sem.at[p])

    def start(copies):
        for copy in copies:
            copy.start()

    def wait(copies):
        for copy in copies:
            copy.wait()

    def begin():
        for p in range(min(ahead, loads)):
            start(heat_copies(p))
        for p in range(loads):
            start(entry_copies(p))
            if p + ahead < loads:
                start(heat_copies(p + ahead))
        heat[:, :, :, 0 : 2 * LANES] = jnp.zeros(heat.shape[:3] + (2 * LANES,), jnp.bfloat16)
        heat[:, :, :, 2 * LANES + columns :] = jnp.zeros(heat.shape[:3] + (LANES,), jnp.bfloat16)

    def prepare(p, seg, t, dv, n, qs):
        row = segments[seg][0]
        own = pl.ds(pl.multiple_of(p * PIECE, PIECE), PIECE)
        cols = pl.ds(pl.multiple_of(2 * LANES + p * PIECE, LANES), PIECE)
        wide = pl.ds(pl.multiple_of(LANES + p * PIECE, LANES), PIECE + 2 * LANES)
        mid = slice(16, 16 + height)

        def put(slot, first, value):
            for q in range(strips):
                t[q, slot, first : first + value.shape[0], :] = value[:, q * LANES : (q + 1) * LANES]

        for q in qs:
            for slot, source in extras.items():
                here = pl.multiple_of(p * PIECE + q * LANES, LANES)
                if source == "before":
                    value = before_ref[row : row + height, pl.ds(here, LANES)].astype(f32) * inside[0]
                elif source == "after":
                    value = after_ref[row : row + height, pl.ds(here, LANES)].astype(f32) * inside[1]
                else:
                    value = heat[seg, source, mid, pl.ds(2 * LANES + here, LANES)].astype(f32)
                t[q, slot, 8 : 8 + height, :] = value
        for first in range(0, share, batch):
            at = n * share + first
            slot0 = centres[0] + stride * at
            if stride == 1:
                window = heat[seg, pl.ds(slot0 - shift, batch), mid, wide].reshape(batch * height, PIECE + 2 * LANES)
            else:
                window = jnp.concatenate([heat[seg, centres[0] - shift + stride * (at + m), mid, wide] for m in range(batch)], axis=0)
            moved = jnp.dot(window, diff[...], preferred_element_type=f32).reshape(batch, height, PIECE)
            for q in range(strips):
                dv[q, pl.ds(at, batch)] = moved[:, :, q * LANES : (q + 1) * LANES]
            for m in range(batch):
                slot = slot0 + stride * m
                z = slot - shift
                layer = z if mode != "ends" else jnp.where(at + m == 0, 0, layers - 1)
                put(slot, 8, heat[seg, z, mid, cols].astype(f32))
                if row == 0:
                    put(slot, 7, rim_rows[0, pl.ds(layer, 1), own])
                else:
                    put(slot, 0, heat[seg, z, 0:16, cols].astype(f32)[8:16])
                if row + height == all_rows:
                    put(slot, 8 + height, rim_rows[1, pl.ds(layer, 1), own])
                else:
                    put(slot, 8 + height, heat[seg, z, 16 + height : 32 + height, cols].astype(f32)[0:8])
                yield

    def looked(index):
        rg, ba = [
            lax.gather(table, index[:, :, None], LANE_LOOKUP, (1, 1), mode=lax.GatherScatterMode.PROMISE_IN_BOUNDS)
            for table in tables
        ]
        return rg.astype(f32), (rg & 0xFFFF).astype(f32), ba.astype(f32), (ba & 0xFFFF).astype(f32) * (4.0 / (sight * LOW_STEPS))

    scale = 0.7 / 9.0
    scales = [scale / (HIGH_STEPS * 65536.0), scale / LOW_STEPS, scale / (HIGH_STEPS * 65536.0)]

    def composite(p, seg, t, dv, qs):
        jobs = [(q, r0) for q in qs for r0 in range(0, height, SUBLANES)]
        size = units_at_once if parts > 1 else len(jobs)
        for group in range(0, len(jobs), size):
            units = []
            for q, r0 in jobs[group : group + size]:
                s = strips * p + q
                units.append(
                    dict(
                        q=q,
                        s=s,
                        r0=r0,
                        cols=pl.ds(pl.multiple_of(s * LANES, LANES), LANES),
                        trans=jnp.ones((SUBLANES, LANES), f32),
                        colors=[jnp.zeros((SUBLANES, LANES), f32) for channel in range(3)],
                        prev=t[q, centres[0] - 1, 8 + r0 : 16 + r0, :],
                        cur=t[q, centres[0], 8 + r0 : 16 + r0, :],
                    )
                )
            for at, slot in enumerate(centres):
                for unit in units:
                    q, r0 = unit["q"], unit["r0"]
                    if mode == "ends" and at == 1:
                        kept = [state_ref[unit["s"], channel, seg * height + r0 : seg * height + r0 + 8, :] for channel in range(4)]
                        unit["colors"] = [old + unit["trans"] * new for old, new in zip(unit["colors"], kept)]
                        unit["trans"] = unit["trans"] * kept[3]
                        unit["prev"], unit["cur"] = t[q, slot - 1, 8 + r0 : 16 + r0, :], t[q, slot, 8 + r0 : 16 + r0, :]
                    nxt = t[q, slot + 1, 8 + r0 : 16 + r0, :]
                    a = nxt - unit["prev"]
                    b = t[q, slot, 9 + r0 : 17 + r0, :] - t[q, slot, 7 + r0 : 15 + r0, :]
                    c = dv[q, at, r0 : r0 + 8, :]
                    m = b + c
                    lit = a + m + m
                    square = (a * a + b * b) + (c * c + 4.0)
                    shade = lit * lit * pl.reciprocal(square, approx=True) + 0.3 / scale
                    red, green, blue, weight = looked(entry[at, seg * height + r0 : seg * height + r0 + 8, unit["cols"]])
                    alpha = weight * pl.reciprocal(jnp.exp2(unit["cur"] * KAPPA) + 1.0, approx=True)
                    part = alpha * unit["trans"]
                    unit["trans"] = unit["trans"] - part
                    shown = shade * part
                    unit["colors"] = [old + new * shown for old, new in zip(unit["colors"], (red, green, blue))]
                    unit["prev"], unit["cur"] = unit["cur"], nxt
                yield
            for pair in range(0, len(units), 2):
                twin = units[pair : pair + 2]
                r0 = out_row + seg * height + twin[0]["r0"]
                for channel in range(4):
                    if mode == "mid":
                        values = [unit["colors"][channel] if channel < 3 else unit["trans"] for unit in twin]
                        out_ref[twin[0]["s"], channel, r0 : r0 + 16, :] = jnp.concatenate(values, axis=0)
                        continue
                    values = [unit["colors"][channel] * scales[channel] if channel < 3 else 1.0 - unit["trans"] for unit in twin]
                    code = jnp.round((jnp.log2(jnp.maximum(jnp.concatenate(values, axis=0), LEAST)) + CENTRE) * STEPS)
                    out_ref[twin[0]["s"], channel, r0 : r0 + 16, :] = code.astype(jnp.int32).astype(jnp.int16)

    def both(first, second):
        def part(n, carry):
            qs = [n] if parts > 1 else list(range(strips))
            following = prepare(*second, n, qs)
            groups = max(height // (SUBLANES * units_at_once), 1) if parts > 1 else 1
            steps = max(groups * len(centres) // share, 1)
            for at, step in enumerate(composite(*first, qs)):
                if at % steps == 0:
                    next(following, None)
            for step in following:
                pass
            return carry

        if parts > 1:
            lax.fori_loop(0, parts, part, 0)
        else:
            part(0, 0)

    def run():
        for p in range(min(ahead, loads)):
            wait(heat_copies(p))
        for n in range(parts):
            for step in prepare(0, 0, ta, da, n, [n] if parts > 1 else list(range(strips))):
                pass

        def body(i, carry):
            @pl.when(i % each == 0)
            def _():
                wait(entry_copies(i // each))

            @pl.when((i % each == 0) & (i // each + ahead < loads))
            def _():
                wait(heat_copies(i // each + ahead))

            both((i, 0, ta, da), (i, 1, tb, db))
            both((i, 1, tb, db), (jnp.minimum(i + 1, count - 1), 0, ta, da))

            @pl.when(i % each == each - 1)
            def _():
                out_copy(i // each).start()

            return carry

        lax.fori_loop(0, count, body, 0)

    def finish():
        for p in range(loads):
            out_copy(p).wait()

    return begin, run, finish


def lookup_words(table_ref, padded):
    padded[...] = jnp.zeros(padded.shape, f32)
    padded[0:4, 0 : table_ref.shape[1]] = table_ref[...]
    tables = []
    for pair in range(2):
        low_half = jnp.round(padded[2 * pair + 1 : 2 * pair + 2, :] * LOW_STEPS)
        high_half = jnp.round(padded[2 * pair : 2 * pair + 1, :] * HIGH_STEPS - low_half * (1.0 / 65536.0))
        words = high_half.astype(jnp.int32) * 65536 + low_half.astype(jnp.int32)
        tables.append(jnp.broadcast_to(words, (SUBLANES, LANES)))
    return tables


def brick(table, heat, entry, groups, sight, before=None, after=None, upper=None, lower=None, state=None):
    layers, all_rows, columns = heat.shape
    pieces = columns // PIECE
    blocks = columns // LANES
    rows_of = [2 * segments[0][1] for segments, mode in groups]
    total = sum(rows_of)
    out_type = f32 if groups[0][1] == "mid" else jnp.int16
    whole = pl.BlockSpec(memory_space=pltpu.HBM)
    inside = pl.BlockSpec(memory_space=pltpu.VMEM)
    given = {"table": (table, whole), "heat": (heat, whole), "entry": (entry, whole)}
    if before is not None:
        given["before"], given["after"] = (before, inside), (after, inside)
    if upper is not None:
        given["upper"], given["lower"] = (upper, inside), (lower, inside)
    if state is not None:
        given["state"] = (state, whole)
    names = list(given)
    common = [
        pltpu.VMEM(table.shape, f32),
        pltpu.VMEM((SUBLANES, LANES), f32),
        pltpu.VMEM((2, layers, columns), f32),
        pltpu.VMEM((PIECE + 2 * LANES, PIECE), jnp.bfloat16),
        pltpu.VMEM((blocks, 4, total, LANES), out_type),
        pltpu.VMEM((blocks, 4, 2 * groups[0][0][0][1] if state is not None else SUBLANES, LANES), f32),
        pltpu.SemaphoreType.DMA,
        pltpu.SemaphoreType.DMA,
    ]
    own = []
    for segments, mode in groups:
        height = segments[0][1]
        held, centres = {"all": (layers, layers), "mid": (layers, layers - 2), "ends": (4, 2)}[mode]
        slots = {"all": layers + 2, "mid": layers, "ends": 6}[mode]
        t = pltpu.VMEM((PIECE // LANES, slots, height + 16, LANES), f32)
        dv = pltpu.VMEM((PIECE // LANES, centres, height, LANES), f32)
        own += [
            pltpu.VMEM((2, held, height + 32, columns + 3 * LANES), jnp.bfloat16),
            pltpu.VMEM((centres, 2 * height, columns), jnp.int32),
            t,
            dv,
            t,
            dv,
            pltpu.SemaphoreType.DMA((4, pieces)),
            pltpu.SemaphoreType.DMA((4, pieces)),
            pltpu.SemaphoreType.DMA((pieces,)),
        ]

    def kernel(*refs):
        ref = dict(zip(names, refs))
        out_hbm = refs[len(names)]
        table_ref, padded, rim_rows, diff, out_ref, state_ref, state_sem, table_sem, *rest = refs[len(names) + 1 :]
        here, side = lax.axis_index("depth"), lax.axis_index("cross")
        flags = [(here > 0).astype(f32), (here < lax.axis_size("depth") - 1).astype(f32)]
        table_copy = pltpu.make_async_copy(ref["table"], table_ref, table_sem)
        table_copy.start()
        tables = []
        if state is not None:
            state_copy = pltpu.make_async_copy(ref["state"], state_ref, state_sem)
            state_copy.start()
        runs, row = [], 0
        for n, (segments, mode) in enumerate(groups):
            runs.append(
                strip_pipeline(tables, rim_rows, flags, ref.get("before"), ref.get("after"), ref["heat"], ref["entry"], state_ref,
                               out_hbm, out_ref, row, diff, *rest[9 * n : 9 * n + 9], segments=segments, mode=mode, sight=sight)
            )
            row += rows_of[n]
        for begin, run, finish in runs:
            begin()
        table_copy.wait()
        tables += lookup_words(table_ref, padded)
        k = lax.broadcasted_iota(jnp.int32, diff.shape, 0) - lax.broadcasted_iota(jnp.int32, diff.shape, 1)
        diff[...] = jnp.where(k == LANES + 1, 1.0, jnp.where(k == LANES - 1, -1.0, 0.0)).astype(jnp.bfloat16)
        if upper is not None:
            rim_rows[0] = ref["upper"][...].astype(f32) * (side > 0).astype(f32)
            rim_rows[1] = ref["lower"][...].astype(f32) * (side < lax.axis_size("cross") - 1).astype(f32)
        if state is not None:
            state_copy.wait()
        for begin, run, finish in runs:
            run()
        for begin, run, finish in runs:
            finish()

    return pl.pallas_call(
        kernel,
        in_specs=[given[name][1] for name in names],
        out_specs=whole,
        out_shape=jax.ShapeDtypeStruct((blocks, 4, total, LANES), out_type),
        scratch_shapes=common + own,
        compiler_params=pltpu.CompilerParams(vmem_limit_bytes=36 * 1024 * 1024),
        name="_".join(mode for segments, mode in groups) + "_layers",
    )(*[given[name][0] for name in names])


def merge_kernel(got, *rest, places):
    out_hbm, image, image_sem = rest[-3:]
    count, channels, rows, lanes = got.shape

    def image_copy(k):
        return pltpu.make_async_copy(image.at[k], out_hbm.at[:, pl.ds(16 * places[k], 16)], image_sem.at[k])

    for k in range(len(places)):
        colors = [jnp.zeros((16, lanes), f32) for channel in range(3)]
        trans = jnp.ones((16, lanes), f32)
        for source in range(count):
            value = [
                jnp.exp2(got[source, channel, 16 * k : 16 * k + 16].astype(f32) * (1.0 / STEPS) - CENTRE)
                for channel in range(4)
            ]
            colors = [old + trans * new for old, new in zip(colors, value)]
            trans = trans - trans * value[3]
        for channel in range(4):
            image[k, channel] = colors[channel] if channel < 3 else 1.0 - trans
        image_copy(k).start()
    for k in range(len(places)):
        image_copy(k).wait()


def merge(got, image, all_rows, places):
    count, channels, rows, lanes = got.shape
    whole = pl.BlockSpec(memory_space=pltpu.HBM)
    operands = [got] if image is None else [got, image]

    def kernel(*refs):
        merge_kernel(*refs, places=places)

    return pl.pallas_call(
        kernel,
        in_specs=[pl.BlockSpec(memory_space=pltpu.VMEM), whole][: len(operands)],
        out_specs=whole,
        out_shape=jax.ShapeDtypeStruct((channels, all_rows, lanes), f32),
        scratch_shapes=[
            pltpu.VMEM((len(places), channels, 16, lanes), f32),
            pltpu.SemaphoreType.DMA((len(places),)),
        ],
        input_output_aliases={} if image is None else {1: 0},
        compiler_params=pltpu.CompilerParams(vmem_limit_bytes=16 * 1024 * 1024),
        name="merge",
    )(*operands)


def local(heat, entry, table):
    count = lax.axis_size("depth")
    sides = lax.axis_size("cross")
    layers, rows, columns = heat.shape
    sight = layers * count

    def turned(value, axis, by):
        size = lax.axis_size(axis)
        return lax.ppermute(value, axis, [(i, (i + by) % size) for i in range(size)])

    before = turned(heat[-1], "depth", 1)
    after = turned(heat[0], "depth", -1)
    upper = turned(heat[:, -1, :], "cross", 1)
    lower = turned(heat[:, 0, :], "cross", -1)

    heat = pltpu.with_memory_space_constraint(heat, pltpu.HBM)
    entry = pltpu.with_memory_space_constraint(entry, pltpu.HBM)
    table = pltpu.with_memory_space_constraint(table, pltpu.HBM)
    centre, inner, outer = ((48, 16), (64, 16)), ((32, 16), (80, 16)), ((0, 32), (96, 32))
    state = brick(table, heat, entry, [(centre, "mid")], sight)
    codes = brick(table, heat, entry, [(centre, "ends"), (inner, "all")], sight, before=before, after=after, upper=upper, lower=lower, state=state)
    codes, before = lax.optimization_barrier((codes, before))
    first = lax.all_to_all(codes, "depth", 0, 0, tiled=True)
    codes = brick(table, heat, entry, [(outer, "all")], sight, before=before, after=after, upper=upper, lower=lower)
    second = lax.all_to_all(codes, "depth", 0, 0, tiled=True)
    image = merge(first, None, rows, (3, 4, 2, 5))
    return merge(second, image, rows, (0, 1, 6, 7))


def solution(mesh):
    in_specs = (P("depth", "cross", None), P("depth", "cross", None), P())
    out_specs = P(None, "cross", "depth")
    return jax.shard_map(local, mesh=mesh, in_specs=in_specs, out_specs=out_specs, check_vma=False)
```

```python
import jax
import jax.numpy as jnp
import numpy as np
from jax import lax
from jax.experimental import pallas as pl
from jax.experimental.pallas import tpu as pltpu
from jax.sharding import PartitionSpec as P

LANES = 128
SUBLANES = 8
PIECE = 256
LOAD = 256
SPLIT = 32
TOGETHER = 8
f32 = jnp.float32
LANE_LOOKUP = lax.GatherDimensionNumbers(
    offset_dims=(),
    collapsed_slice_dims=(1,),
    start_index_map=(1,),
    operand_batching_dims=(0,),
    start_indices_batching_dims=(0,),
)
KAPPA = -2.0 / float(np.log(2.0))
HIGH_STEPS = 32766.0
LOW_STEPS = 65535.0
CENTRE = 16.0
STEPS = 2340.0
LEAST = 2.0**-29.9


def strip_pipeline(tables, rim_rows, inside, before_ref, after_ref, heat_hbm, entry_hbm, state_ref, out_hbm, out_ref, out_row, weights, heat, entry,
                   rows_by, first_set, second_set, heat_sem, entry_sem, out_sem, *, segments, mode, sight):
    all_rows, columns = heat_hbm.shape[1:]
    layers = heat_hbm.shape[0]
    height = segments[0][1]
    count = columns // PIECE
    strips = PIECE // LANES
    centres = {"all": list(range(1, layers + 1)), "mid": list(range(1, layers - 1)), "ends": [1, 4]}[mode]
    shift = 0 if mode == "mid" else 1
    stride = centres[1] - centres[0]
    parts = strips if height > SPLIT else 1
    share = len(centres) // parts
    batch = min(share, 128 // height)
    while share % batch or (stride > 1 and batch > 1):
        batch -= 1

    load = columns if mode == "ends" else LOAD
    loads, each = columns // load, load // PIECE
    ahead = 2 if each == 1 else 1
    adjacent = segments[1][0] == segments[0][0] + height
    blocks_of_rows = [(segments[0][0], 0, 2 * height)] if adjacent else [(row, k * height, height) for k, (row, _) in enumerate(segments)]

    def heat_copies(p):
        cols = pl.ds(pl.multiple_of(p * load, load), load)
        into = pl.ds(pl.multiple_of(2 * LANES + p * load, LANES), load)
        found = []
        for k, (row, _) in enumerate(segments):
            low, high = max(row - 16, 0), min(row + height + 16, all_rows)
            target = pl.ds(16 - (row - low), high - low)
            pairs = [(0, 0, 2), (layers - 2, 2, 2)] if mode == "ends" else [(0, 0, layers)]
            for n, (source, first, size) in enumerate(pairs):
                found.append(
                    pltpu.make_async_copy(
                        heat_hbm.at[pl.ds(source, size), pl.ds(low, high - low), cols],
                        heat.at[k, pl.ds(first, size), target, into],
                        heat_sem.at[2 * k + n, p],
                    )
                )
        return found

    def entry_copies(p):
        cols = pl.ds(pl.multiple_of(p * load, load), load)
        found = []
        for k, (row, own, size) in enumerate(blocks_of_rows):
            if mode == "ends":
                pairs = [(0, 0, 1), (layers - 1, 1, 1)]
            else:
                pairs = [(1 if mode == "mid" else 0, 0, len(centres))]
            for n, (source, first, deep) in enumerate(pairs):
                found.append(
                    pltpu.make_async_copy(
                        entry_hbm.at[pl.ds(source, deep), pl.ds(row, size), cols],
                        entry.at[pl.ds(first, deep), pl.ds(own, size), cols],
                        entry_sem.at[2 * k + n, p],
                    )
                )
        return found

    def out_copy(p):
        here = pl.ds(p * (load // LANES), load // LANES)
        rows = pl.ds(out_row, 2 * height)
        return pltpu.make_async_copy(out_ref.at[here, :, rows], out_hbm.at[here, :, rows], out_sem.at[p])

    def start(copies):
        for copy in copies:
            copy.start()

    def wait(copies):
        for copy in copies:
            copy.wait()

    def begin():
        for p in range(min(ahead, loads)):
            start(heat_copies(p))
        for p in range(loads):
            start(entry_copies(p))
            if p + ahead < loads:
                start(heat_copies(p + ahead))
        heat[:, :, :, 0 : 2 * LANES] = jnp.zeros(heat.shape[:3] + (2 * LANES,), jnp.bfloat16)
        heat[:, :, :, 2 * LANES + columns :] = jnp.zeros(heat.shape[:3] + (LANES,), jnp.bfloat16)
        k = lax.broadcasted_iota(jnp.int32, rows_by.shape, 1) - lax.broadcasted_iota(jnp.int32, rows_by.shape, 0)
        rows_by[...] = jnp.where(k == 17, 1.0, jnp.where(k == 15, -1.0, 0.0)).astype(jnp.bfloat16)
        across = slice(2 * LANES, 2 * LANES + columns)
        for seg, (row, _) in enumerate(segments):
            for side, at_edge, first in ((0, row == 0, 0), (1, row + height == all_rows, 16 + height)):
                if at_edge:
                    for z in range(layers):
                        rim = jnp.broadcast_to(rim_rows[side, z : z + 1, :], (16, columns))
                        heat[seg, z, first : first + 16, across] = rim.astype(jnp.bfloat16)

    def prepare(p, seg, kept, n):
        cols = pl.ds(pl.multiple_of(2 * LANES + p * PIECE, LANES), PIECE)
        wide = pl.ds(pl.multiple_of(LANES + p * PIECE, LANES), PIECE + 2 * LANES)
        mid = slice(16, 16 + height)
        for first in range(0, share, batch):
            at = n * share + first
            own = centres[0] - shift + stride * at
            window = heat[seg, pl.ds(own, batch), mid, wide].reshape(batch * height, PIECE + 2 * LANES)
            moved = jnp.dot(window, weights[...], preferred_element_type=f32).reshape(batch, height, PIECE)
            for q in range(strips):
                kept[1][q, pl.ds(at, batch)] = moved[:, :, q * LANES : (q + 1) * LANES]
            yield
            for m in range(batch):
                moved = jnp.dot(rows_by[...], heat[seg, own + m, :, cols], preferred_element_type=f32)
                for q in range(strips):
                    kept[0][q, at + m] = moved[:, q * LANES : (q + 1) * LANES]
                yield

    def looked(index):
        rg, ba = [
            lax.gather(table, index[:, :, None], LANE_LOOKUP, (1, 1), mode=lax.GatherScatterMode.PROMISE_IN_BOUNDS)
            for table in tables
        ]
        return rg.astype(f32), (rg & 0xFFFF).astype(f32), ba.astype(f32), (ba & 0xFFFF).astype(f32) * (4.0 / (sight * LOW_STEPS))

    scale = 0.7 / 9.0
    scales = [scale / (HIGH_STEPS * 65536.0), scale / LOW_STEPS, scale / (HIGH_STEPS * 65536.0)]

    def composite(p, seg, kept, qs):
        jobs = [(q, r0) for q in qs for r0 in range(0, height, SUBLANES)]
        size = min(TOGETHER, len(jobs))
        for group in range(0, len(jobs), size):
            units = []
            for q, r0 in jobs[group : group + size]:
                s = strips * p + q
                units.append(
                    dict(
                        q=q,
                        s=s,
                        r0=r0,
                        cols=pl.ds(pl.multiple_of(s * LANES, LANES), LANES),
                        trans=jnp.ones((SUBLANES, LANES), f32),
                        colors=[jnp.zeros((SUBLANES, LANES), f32) for channel in range(3)],
                    )
                )
            def layer(slot, unit):
                r0 = unit["r0"]
                rows = pl.ds(segments[seg][0] + r0, 16)
                if slot == 0 and shift:
                    return before_ref[rows, unit["cols"]].astype(f32) * inside[0]
                if slot == centres[-1] + 1 and shift:
                    return after_ref[rows, unit["cols"]].astype(f32) * inside[1]
                lanes = pl.ds(pl.multiple_of((unit["s"] + 2) * LANES, LANES), LANES)
                return heat[seg, slot - shift, 16 + r0 : 32 + r0, lanes].astype(f32)

            for at, slot in enumerate(centres):
                for number, unit in enumerate(units):
                    q, r0 = unit["q"], unit["r0"]
                    if number % 2 == 0:
                        if at == 0 or stride > 1:
                            prev, cur = layer(slot - 1, unit), layer(slot, unit)
                        else:
                            prev, cur = unit["layers"]
                        nxt = layer(slot + 1, unit)
                        unit["layers"] = cur, nxt
                        steps = nxt - prev
                    half = slice(0, 8) if number % 2 == 0 else slice(8, 16)
                    if mode == "ends" and at == 1:
                        old = [state_ref[unit["s"], channel, seg * height + r0 : seg * height + r0 + 8, :] for channel in range(4)]
                        unit["colors"] = [held + unit["trans"] * new for held, new in zip(unit["colors"], old)]
                        unit["trans"] = unit["trans"] * old[3]
                    a = steps[half]
                    b, c = [values[q, at, r0 : r0 + 8, :] for values in kept]
                    m = b + c
                    lit = a + m + m
                    square = (a * a + b * b) + (c * c + 4.0)
                    shade = lit * lit * pl.reciprocal(square, approx=True) + 0.3 / scale
                    red, green, blue, weight = looked(entry[at, seg * height + r0 : seg * height + r0 + 8, unit["cols"]])
                    alpha = weight * pl.reciprocal(jnp.exp2(cur[half] * KAPPA) + 1.0, approx=True)
                    part = alpha * unit["trans"]
                    unit["trans"] = unit["trans"] - part
                    shown = shade * part
                    unit["colors"] = [old + new * shown for old, new in zip(unit["colors"], (red, green, blue))]
                yield
            for pair in range(0, len(units), 2):
                twin = units[pair : pair + 2]
                r0 = out_row + seg * height + twin[0]["r0"]
                for channel in range(4):
                    if mode == "mid":
                        values = [unit["colors"][channel] if channel < 3 else unit["trans"] for unit in twin]
                        out_ref[twin[0]["s"], channel, r0 : r0 + 16, :] = jnp.concatenate(values, axis=0)
                        continue
                    values = [unit["colors"][channel] * scales[channel] if channel < 3 else 1.0 - unit["trans"] for unit in twin]
                    code = jnp.round((jnp.log2(jnp.maximum(jnp.concatenate(values, axis=0), LEAST)) + CENTRE) * STEPS)
                    out_ref[twin[0]["s"], channel, r0 : r0 + 16, :] = code.astype(jnp.int32).astype(jnp.int16)

    def both(first, second):
        def part(n, carry):
            qs = [n] if parts > 1 else list(range(strips))
            following = prepare(*second, n)
            groups = max(len(qs) * height // (SUBLANES * TOGETHER), 1)
            steps = max(groups * len(centres) // (share // batch * (batch + 1)), 1)
            for at, step in enumerate(composite(*first, qs)):
                if at % steps == 0:
                    next(following, None)
            for step in following:
                pass
            return carry

        if parts > 1:
            lax.fori_loop(0, parts, part, 0)
        else:
            part(0, 0)

    def run():
        for p in range(min(ahead, loads)):
            wait(heat_copies(p))
        for n in range(parts):
            for step in prepare(0, 0, first_set, n):
                pass

        def body(i, carry):
            @pl.when(i % each == 0)
            def _():
                wait(entry_copies(i // each))

            @pl.when((i % each == 0) & (i // each + ahead < loads))
            def _():
                wait(heat_copies(i // each + ahead))

            both((i, 0, first_set), (i, 1, second_set))
            both((i, 1, second_set), (jnp.minimum(i + 1, count - 1), 0, first_set))

            @pl.when(i % each == each - 1)
            def _():
                out_copy(i // each).start()

            return carry

        lax.fori_loop(0, count, body, 0)

    def finish():
        for p in range(loads):
            out_copy(p).wait()

    return begin, run, finish


def lookup_words(table_ref, padded):
    padded[...] = jnp.zeros(padded.shape, f32)
    padded[0:4, 0 : table_ref.shape[1]] = table_ref[...]
    tables = []
    for pair in range(2):
        low_half = jnp.round(padded[2 * pair + 1 : 2 * pair + 2, :] * LOW_STEPS)
        high_half = jnp.round(padded[2 * pair : 2 * pair + 1, :] * HIGH_STEPS - low_half * (1.0 / 65536.0))
        words = high_half.astype(jnp.int32) * 65536 + low_half.astype(jnp.int32)
        tables.append(jnp.broadcast_to(words, (SUBLANES, LANES)))
    return tables


def brick(table, heat, entry, groups, sight, before=None, after=None, upper=None, lower=None, state=None):
    layers, all_rows, columns = heat.shape
    pieces = columns // PIECE
    blocks = columns // LANES
    rows_of = [2 * segments[0][1] for segments, mode in groups]
    total = sum(rows_of)
    out_type = f32 if groups[0][1] == "mid" else jnp.int16
    whole = pl.BlockSpec(memory_space=pltpu.HBM)
    inside = pl.BlockSpec(memory_space=pltpu.VMEM)
    given = {"table": (table, whole), "heat": (heat, whole), "entry": (entry, whole)}
    if before is not None:
        given["before"], given["after"] = (before, inside), (after, inside)
    if upper is not None:
        given["upper"], given["lower"] = (upper, inside), (lower, inside)
    if state is not None:
        given["state"] = (state, whole)
    names = list(given)
    common = [
        pltpu.VMEM(table.shape, f32),
        pltpu.VMEM((SUBLANES, LANES), f32),
        pltpu.VMEM((2, layers, columns), f32),
        pltpu.VMEM((PIECE + 2 * LANES, PIECE), jnp.bfloat16),
        pltpu.VMEM((blocks, 4, total, LANES), out_type),
        pltpu.VMEM((blocks, 4, 2 * groups[0][0][0][1] if state is not None else SUBLANES, LANES), f32),
        pltpu.SemaphoreType.DMA,
        pltpu.SemaphoreType.DMA,
    ]
    own = []
    for segments, mode in groups:
        height = segments[0][1]
        held, centres = {"all": (layers, layers), "mid": (layers, layers - 2), "ends": (4, 2)}[mode]
        kept = [pltpu.VMEM((PIECE // LANES, centres, height, LANES), f32) for number in range(2)]
        own += [
            pltpu.VMEM((2, held, height + 32, columns + 3 * LANES), jnp.bfloat16),
            pltpu.VMEM((centres, 2 * height, columns), jnp.int32),
            pltpu.VMEM((height, height + 32), jnp.bfloat16),
            kept,
            kept,
            pltpu.SemaphoreType.DMA((4, pieces)),
            pltpu.SemaphoreType.DMA((4, pieces)),
            pltpu.SemaphoreType.DMA((pieces,)),
        ]

    def kernel(*refs):
        ref = dict(zip(names, refs))
        out_hbm = refs[len(names)]
        table_ref, padded, rim_rows, weights, out_ref, state_ref, state_sem, table_sem, *rest = refs[len(names) + 1 :]
        here, side = lax.axis_index("depth"), lax.axis_index("cross")
        flags = [(here > 0).astype(f32), (here < lax.axis_size("depth") - 1).astype(f32)]
        table_copy = pltpu.make_async_copy(ref["table"], table_ref, table_sem)
        table_copy.start()
        tables = []
        if state is not None:
            state_copy = pltpu.make_async_copy(ref["state"], state_ref, state_sem)
            state_copy.start()
        runs, row = [], 0
        for n, (segments, mode) in enumerate(groups):
            runs.append(
                strip_pipeline(tables, rim_rows, flags, ref.get("before"), ref.get("after"), ref["heat"], ref["entry"], state_ref,
                               out_hbm, out_ref, row, weights, *rest[8 * n : 8 * n + 8], segments=segments, mode=mode, sight=sight)
            )
            row += rows_of[n]
        if upper is not None:
            rim_rows[0] = ref["upper"][...].astype(f32) * (side > 0).astype(f32)
            rim_rows[1] = ref["lower"][...].astype(f32) * (side < lax.axis_size("cross") - 1).astype(f32)
        for begin, run, finish in runs:
            begin()
        k = lax.broadcasted_iota(jnp.int32, weights.shape, 0) - lax.broadcasted_iota(jnp.int32, weights.shape, 1)
        weights[...] = jnp.where(k == LANES + 1, 1.0, jnp.where(k == LANES - 1, -1.0, 0.0)).astype(jnp.bfloat16)
        table_copy.wait()
        tables += lookup_words(table_ref, padded)
        if state is not None:
            state_copy.wait()
        for begin, run, finish in runs:
            run()
        for begin, run, finish in runs:
            finish()

    return pl.pallas_call(
        kernel,
        in_specs=[given[name][1] for name in names],
        out_specs=whole,
        out_shape=jax.ShapeDtypeStruct((blocks, 4, total, LANES), out_type),
        scratch_shapes=common + own,
        compiler_params=pltpu.CompilerParams(vmem_limit_bytes=36 * 1024 * 1024),
        name="_".join(mode for segments, mode in groups) + "_layers",
    )(*[given[name][0] for name in names])


def merge_kernel(got, *rest, places):
    out_hbm, image, image_sem = rest[-3:]
    count, channels, rows, lanes = got.shape

    def image_copy(k):
        return pltpu.make_async_copy(image.at[k], out_hbm.at[:, pl.ds(16 * places[k], 16)], image_sem.at[k])

    for k in range(len(places)):
        colors = [jnp.zeros((16, lanes), f32) for channel in range(3)]
        trans = jnp.ones((16, lanes), f32)
        for source in range(count):
            value = [
                jnp.exp2(got[source, channel, 16 * k : 16 * k + 16].astype(f32) * (1.0 / STEPS) - CENTRE)
                for channel in range(4)
            ]
            colors = [old + trans * new for old, new in zip(colors, value)]
            trans = trans - trans * value[3]
        for channel in range(4):
            image[k, channel] = colors[channel] if channel < 3 else 1.0 - trans
        image_copy(k).start()
    for k in range(len(places)):
        image_copy(k).wait()


def merge(got, image, all_rows, places):
    count, channels, rows, lanes = got.shape
    whole = pl.BlockSpec(memory_space=pltpu.HBM)
    operands = [got] if image is None else [got, image]

    def kernel(*refs):
        merge_kernel(*refs, places=places)

    return pl.pallas_call(
        kernel,
        in_specs=[pl.BlockSpec(memory_space=pltpu.VMEM), whole][: len(operands)],
        out_specs=whole,
        out_shape=jax.ShapeDtypeStruct((channels, all_rows, lanes), f32),
        scratch_shapes=[
            pltpu.VMEM((len(places), channels, 16, lanes), f32),
            pltpu.SemaphoreType.DMA((len(places),)),
        ],
        input_output_aliases={} if image is None else {1: 0},
        compiler_params=pltpu.CompilerParams(vmem_limit_bytes=16 * 1024 * 1024),
        name="merge",
    )(*operands)


def local(heat, entry, table):
    count = lax.axis_size("depth")
    sides = lax.axis_size("cross")
    layers, rows, columns = heat.shape
    sight = layers * count

    def turned(value, axis, by):
        size = lax.axis_size(axis)
        return lax.ppermute(value, axis, [(i, (i + by) % size) for i in range(size)])

    before = turned(heat[-1], "depth", 1)
    after = turned(heat[0], "depth", -1)
    upper = turned(heat[:, -1, :], "cross", 1)
    lower = turned(heat[:, 0, :], "cross", -1)

    heat = pltpu.with_memory_space_constraint(heat, pltpu.HBM)
    entry = pltpu.with_memory_space_constraint(entry, pltpu.HBM)
    table = pltpu.with_memory_space_constraint(table, pltpu.HBM)
    centre, inner, outer = ((48, 16), (64, 16)), ((32, 16), (80, 16)), ((0, 32), (96, 32))
    state = brick(table, heat, entry, [(centre, "mid")], sight)
    codes = brick(table, heat, entry, [(centre, "ends"), (inner, "all")], sight, before=before, after=after, upper=upper, lower=lower, state=state)
    codes, before = lax.optimization_barrier((codes, before))
    first = lax.all_to_all(codes, "depth", 0, 0, tiled=True)
    codes = brick(table, heat, entry, [(outer, "all")], sight, before=before, after=after, upper=upper, lower=lower)
    second = lax.all_to_all(codes, "depth", 0, 0, tiled=True)
    image = merge(first, None, rows, (3, 4, 2, 5))
    return merge(second, image, rows, (0, 1, 6, 7))


def solution(mesh):
    in_specs = (P("depth", "cross", None), P("depth", "cross", None), P())
    out_specs = P(None, "cross", "depth")
    return jax.shard_map(local, mesh=mesh, in_specs=in_specs, out_specs=out_specs, check_vma=False)
```

```python
import jax
import jax.numpy as jnp
import numpy as np
from jax import lax
from jax.experimental import pallas as pl
from jax.experimental.pallas import tpu as pltpu
from jax.sharding import PartitionSpec as P

LANES = 128
SUBLANES = 8
PIECE = 256
LOAD = 256
SPLIT = 32
TOGETHER = 8
f32 = jnp.float32
LANE_LOOKUP = lax.GatherDimensionNumbers(
    offset_dims=(),
    collapsed_slice_dims=(1,),
    start_index_map=(1,),
    operand_batching_dims=(0,),
    start_indices_batching_dims=(0,),
)
KAPPA = -2.0 / float(np.log(2.0))
HIGH_STEPS = 32766.0
LOW_STEPS = 65535.0
CENTRE = 16.0
STEPS = 2340.0
LEAST = 2.0**-29.9


def strip_pipeline(tables, rim_rows, inside, before_ref, after_ref, heat_hbm, entry_hbm, state_ref, out_hbm, out_ref, out_row, weights, heat, entry,
                   rows_by, first_set, second_set, heat_sem, entry_sem, out_sem, *, segments, mode, sight):
    all_rows, columns = heat_hbm.shape[1:]
    layers = heat_hbm.shape[0]
    height = segments[0][1]
    count = columns // PIECE
    strips = PIECE // LANES
    centres = {"all": list(range(1, layers + 1)), "mid": list(range(1, layers - 1)), "ends": [1, 4]}[mode]
    shift = 0 if mode == "mid" else 1
    stride = centres[1] - centres[0]
    parts = strips if height > SPLIT else 1
    share = len(centres) // parts
    batch = min(share, 128 // height)
    while share % batch or (stride > 1 and batch > 1):
        batch -= 1

    load = 2 * LOAD if mode == "ends" else LOAD
    loads, each = columns // load, load // PIECE
    ahead = 2 if each == 1 else 1
    adjacent = segments[1][0] == segments[0][0] + height
    blocks_of_rows = [(segments[0][0], 0, 2 * height)] if adjacent else [(row, k * height, height) for k, (row, _) in enumerate(segments)]

    def heat_copies(p):
        cols = pl.ds(pl.multiple_of(p * load, load), load)
        into = pl.ds(pl.multiple_of(2 * LANES + p * load, LANES), load)
        found = []
        for k, (row, _) in enumerate(segments):
            low, high = max(row - 16, 0), min(row + height + 16, all_rows)
            target = pl.ds(16 - (row - low), high - low)
            pairs = [(0, 0, 2), (layers - 2, 2, 2)] if mode == "ends" else [(0, 0, layers)]
            for n, (source, first, size) in enumerate(pairs):
                found.append(
                    pltpu.make_async_copy(
                        heat_hbm.at[pl.ds(source, size), pl.ds(low, high - low), cols],
                        heat.at[k, pl.ds(first, size), target, into],
                        heat_sem.at[2 * k + n, p],
                    )
                )
        return found

    def entry_copies(p):
        cols = pl.ds(pl.multiple_of(p * load, load), load)
        found = []
        for k, (row, own, size) in enumerate(blocks_of_rows):
            if mode == "ends":
                pairs = [(0, 0, 1), (layers - 1, 1, 1)]
            else:
                pairs = [(1 if mode == "mid" else 0, 0, len(centres))]
            for n, (source, first, deep) in enumerate(pairs):
                found.append(
                    pltpu.make_async_copy(
                        entry_hbm.at[pl.ds(source, deep), pl.ds(row, size), cols],
                        entry.at[pl.ds(first, deep), pl.ds(own, size), cols],
                        entry_sem.at[2 * k + n, p],
                    )
                )
        return found

    def out_copy(p):
        here = pl.ds(p * (load // LANES), load // LANES)
        rows = pl.ds(out_row, 2 * height)
        return pltpu.make_async_copy(out_ref.at[here, :, rows], out_hbm.at[here, :, rows], out_sem.at[p])

    def start(copies):
        for copy in copies:
            copy.start()

    def wait(copies):
        for copy in copies:
            copy.wait()

    def begin():
        for p in range(min(ahead, loads)):
            start(heat_copies(p))
        for p in range(loads):
            start(entry_copies(p))
            if p + ahead < loads:
                start(heat_copies(p + ahead))
        heat[:, :, :, 0 : 2 * LANES] = jnp.zeros(heat.shape[:3] + (2 * LANES,), jnp.bfloat16)
        heat[:, :, :, 2 * LANES + columns :] = jnp.zeros(heat.shape[:3] + (LANES,), jnp.bfloat16)
        k = lax.broadcasted_iota(jnp.int32, rows_by.shape, 1) - lax.broadcasted_iota(jnp.int32, rows_by.shape, 0)
        rows_by[...] = jnp.where(k == 17, 1.0, jnp.where(k == 15, -1.0, 0.0)).astype(jnp.bfloat16)
        across = slice(2 * LANES, 2 * LANES + columns)
        for seg, (row, _) in enumerate(segments):
            for side, at_edge, first in ((0, row == 0, 0), (1, row + height == all_rows, 16 + height)):
                if at_edge:
                    for z in range(layers):
                        rim = jnp.broadcast_to(rim_rows[side, z : z + 1, :], (16, columns))
                        heat[seg, z, first : first + 16, across] = rim.astype(jnp.bfloat16)

    def prepare(p, seg, kept, n):
        cols = pl.ds(pl.multiple_of(2 * LANES + p * PIECE, LANES), PIECE)
        wide = pl.ds(pl.multiple_of(LANES + p * PIECE, LANES), PIECE + 2 * LANES)
        mid = slice(16, 16 + height)
        for first in range(0, share, batch):
            at = n * share + first
            own = centres[0] - shift + stride * at
            window = heat[seg, pl.ds(own, batch), mid, wide].reshape(batch * height, PIECE + 2 * LANES)
            moved = jnp.dot(window, weights[...], preferred_element_type=f32).reshape(batch, height, PIECE)
            for q in range(strips):
                kept[1][q, pl.ds(at, batch)] = moved[:, :, q * LANES : (q + 1) * LANES]
            yield
            for m in range(batch):
                moved = jnp.dot(rows_by[...], heat[seg, own + m, :, cols], preferred_element_type=f32)
                for q in range(strips):
                    kept[0][q, at + m] = moved[:, q * LANES : (q + 1) * LANES]
                yield

    def looked(index):
        rg, ba = [
            lax.gather(table, index[:, :, None], LANE_LOOKUP, (1, 1), mode=lax.GatherScatterMode.PROMISE_IN_BOUNDS)
            for table in tables
        ]
        return rg.astype(f32), (rg & 0xFFFF).astype(f32), ba.astype(f32), (ba & 0xFFFF).astype(f32) * (4.0 / (sight * LOW_STEPS))

    scale = 0.7 / 9.0
    scales = [scale / (HIGH_STEPS * 65536.0), scale / LOW_STEPS, scale / (HIGH_STEPS * 65536.0)]

    def composite(p, seg, kept, qs):
        jobs = [(q, r0) for q in qs for r0 in range(0, height, SUBLANES)]
        size = min(TOGETHER, len(jobs))
        for group in range(0, len(jobs), size):
            units = []
            for q, r0 in jobs[group : group + size]:
                s = strips * p + q
                units.append(
                    dict(
                        q=q,
                        s=s,
                        r0=r0,
                        cols=pl.ds(pl.multiple_of(s * LANES, LANES), LANES),
                        trans=jnp.ones((SUBLANES, LANES), f32),
                        colors=[jnp.zeros((SUBLANES, LANES), f32) for channel in range(3)],
                    )
                )
            def layer(slot, unit):
                r0 = unit["r0"]
                rows = pl.ds(segments[seg][0] + r0, 16)
                if slot == 0 and shift:
                    return before_ref[rows, unit["cols"]].astype(f32) * inside[0]
                if slot == centres[-1] + 1 and shift:
                    return after_ref[rows, unit["cols"]].astype(f32) * inside[1]
                lanes = pl.ds(pl.multiple_of((unit["s"] + 2) * LANES, LANES), LANES)
                return heat[seg, slot - shift, 16 + r0 : 32 + r0, lanes].astype(f32)

            for at, slot in enumerate(centres):
                for number, unit in enumerate(units):
                    q, r0 = unit["q"], unit["r0"]
                    if number % 2 == 0:
                        if at == 0 or stride > 1:
                            prev, cur = layer(slot - 1, unit), layer(slot, unit)
                        else:
                            prev, cur = unit["layers"]
                        nxt = layer(slot + 1, unit)
                        unit["layers"] = cur, nxt
                        steps = nxt - prev
                    half = slice(0, 8) if number % 2 == 0 else slice(8, 16)
                    if mode == "ends" and at == 1:
                        old = [state_ref[unit["s"], channel, seg * height + r0 : seg * height + r0 + 8, :] for channel in range(4)]
                        unit["colors"] = [held + unit["trans"] * new for held, new in zip(unit["colors"], old)]
                        unit["trans"] = unit["trans"] * old[3]
                    a = steps[half]
                    b, c = [values[q, at, r0 : r0 + 8, :] for values in kept]
                    m = b + c
                    lit = a + m + m
                    square = (a * a + b * b) + (c * c + 4.0)
                    shade = lit * lit * pl.reciprocal(square, approx=True) + 0.3 / scale
                    red, green, blue, weight = looked(entry[at, seg * height + r0 : seg * height + r0 + 8, unit["cols"]])
                    alpha = weight * pl.reciprocal(jnp.exp2(cur[half] * KAPPA) + 1.0, approx=True)
                    part = alpha * unit["trans"]
                    unit["trans"] = unit["trans"] - part
                    shown = shade * part
                    unit["colors"] = [old + new * shown for old, new in zip(unit["colors"], (red, green, blue))]
                yield
            for pair in range(0, len(units), 2):
                twin = units[pair : pair + 2]
                r0 = out_row + seg * height + twin[0]["r0"]
                for channel in range(4):
                    if mode == "mid":
                        values = [unit["colors"][channel] if channel < 3 else unit["trans"] for unit in twin]
                        out_ref[twin[0]["s"], channel, r0 : r0 + 16, :] = jnp.concatenate(values, axis=0)
                        continue
                    values = [unit["colors"][channel] * scales[channel] if channel < 3 else 1.0 - unit["trans"] for unit in twin]
                    code = jnp.round((jnp.log2(jnp.maximum(jnp.concatenate(values, axis=0), LEAST)) + CENTRE) * STEPS)
                    out_ref[twin[0]["s"], channel, r0 : r0 + 16, :] = code.astype(jnp.int32).astype(jnp.int16)

    def both(first, second):
        def part(n, carry):
            qs = [n] if parts > 1 else list(range(strips))
            following = prepare(*second, n)
            groups = max(len(qs) * height // (SUBLANES * TOGETHER), 1)
            steps = max(groups * len(centres) // (share // batch * (batch + 1)), 1)
            for at, step in enumerate(composite(*first, qs)):
                if at % steps == 0:
                    next(following, None)
            for step in following:
                pass
            return carry

        if parts > 1:
            lax.fori_loop(0, parts, part, 0)
        else:
            part(0, 0)

    def run():
        for p in range(min(ahead, loads)):
            wait(heat_copies(p))
        for n in range(parts):
            for step in prepare(0, 0, first_set, n):
                pass

        def body(i, carry):
            @pl.when(i % each == 0)
            def _():
                wait(entry_copies(i // each))

            @pl.when((i % each == 0) & (i // each + ahead < loads))
            def _():
                wait(heat_copies(i // each + ahead))

            both((i, 0, first_set), (i, 1, second_set))
            both((i, 1, second_set), (jnp.minimum(i + 1, count - 1), 0, first_set))

            if out_hbm is not None:

                @pl.when(i % each == each - 1)
                def _():
                    out_copy(i // each).start()

            return carry

        lax.fori_loop(0, count, body, 0)

    def finish():
        for p in range(loads if out_hbm is not None else 0):
            out_copy(p).wait()

    return begin, run, finish


def lookup_words(table_ref, padded):
    padded[...] = jnp.zeros(padded.shape, f32)
    padded[0:4, 0 : table_ref.shape[1]] = table_ref[...]
    tables = []
    for pair in range(2):
        low_half = jnp.round(padded[2 * pair + 1 : 2 * pair + 2, :] * LOW_STEPS)
        high_half = jnp.round(padded[2 * pair : 2 * pair + 1, :] * HIGH_STEPS - low_half * (1.0 / 65536.0))
        words = high_half.astype(jnp.int32) * 65536 + low_half.astype(jnp.int32)
        tables.append(jnp.broadcast_to(words, (SUBLANES, LANES)))
    return tables


def brick(table, heat, entry, groups, sight, before=None, after=None, upper=None, lower=None, state=None):
    layers, all_rows, columns = heat.shape
    pieces = columns // PIECE
    blocks = columns // LANES
    rows_of = [2 * segments[0][1] for segments, mode in groups]
    total = sum(rows_of)
    direct = groups[0][1] == "mid"
    out_type = f32 if direct else jnp.int16
    whole = pl.BlockSpec(memory_space=pltpu.HBM)
    inside = pl.BlockSpec(memory_space=pltpu.VMEM)
    given = {"table": (table, whole), "heat": (heat, whole), "entry": (entry, whole)}
    if before is not None:
        given["before"], given["after"] = (before, inside), (after, inside)
    if upper is not None:
        given["upper"], given["lower"] = (upper, inside), (lower, inside)
    if state is not None:
        given["state"] = (state, inside)
    names = list(given)
    common = [
        pltpu.VMEM(table.shape, f32),
        pltpu.VMEM((SUBLANES, LANES), f32),
        pltpu.VMEM((2, layers, columns), f32),
        pltpu.VMEM((PIECE + 2 * LANES, PIECE), jnp.bfloat16),
        pltpu.VMEM((SUBLANES, LANES) if direct else (blocks, 4, total, LANES), out_type),
        pltpu.SemaphoreType.DMA,
    ]
    own = []
    for segments, mode in groups:
        height = segments[0][1]
        held, centres = {"all": (layers, layers), "mid": (layers, layers - 2), "ends": (4, 2)}[mode]
        kept = [pltpu.VMEM((PIECE // LANES, centres, height, LANES), f32) for number in range(2)]
        own += [
            pltpu.VMEM((2, held, height + 32, columns + 3 * LANES), jnp.bfloat16),
            pltpu.VMEM((centres, 2 * height, columns), jnp.int32),
            pltpu.VMEM((height, height + 32), jnp.bfloat16),
            kept,
            kept,
            pltpu.SemaphoreType.DMA((4, pieces)),
            pltpu.SemaphoreType.DMA((4, pieces)),
            pltpu.SemaphoreType.DMA((pieces,)),
        ]

    def kernel(*refs):
        ref = dict(zip(names, refs))
        out_hbm = refs[len(names)]
        table_ref, padded, rim_rows, weights, out_ref, table_sem, *rest = refs[len(names) + 1 :]
        if direct:
            out_hbm, out_ref = None, out_hbm
        here, side = lax.axis_index("depth"), lax.axis_index("cross")
        flags = [(here > 0).astype(f32), (here < lax.axis_size("depth") - 1).astype(f32)]
        table_copy = pltpu.make_async_copy(ref["table"], table_ref, table_sem)
        table_copy.start()
        tables = []
        runs, row = [], 0
        for n, (segments, mode) in enumerate(groups):
            runs.append(
                strip_pipeline(tables, rim_rows, flags, ref.get("before"), ref.get("after"), ref["heat"], ref["entry"], ref.get("state"),
                               out_hbm, out_ref, row, weights, *rest[8 * n : 8 * n + 8], segments=segments, mode=mode, sight=sight)
            )
            row += rows_of[n]
        if upper is not None:
            rim_rows[0] = ref["upper"][...].astype(f32) * (side > 0).astype(f32)
            rim_rows[1] = ref["lower"][...].astype(f32) * (side < lax.axis_size("cross") - 1).astype(f32)
        for begin, run, finish in runs:
            begin()
        k = lax.broadcasted_iota(jnp.int32, weights.shape, 0) - lax.broadcasted_iota(jnp.int32, weights.shape, 1)
        weights[...] = jnp.where(k == LANES + 1, 1.0, jnp.where(k == LANES - 1, -1.0, 0.0)).astype(jnp.bfloat16)
        table_copy.wait()
        tables += lookup_words(table_ref, padded)
        for begin, run, finish in runs:
            run()
        for begin, run, finish in runs:
            finish()

    return pl.pallas_call(
        kernel,
        in_specs=[given[name][1] for name in names],
        out_specs=inside if direct else whole,
        out_shape=jax.ShapeDtypeStruct((blocks, 4, total, LANES), out_type),
        scratch_shapes=common + own,
        compiler_params=pltpu.CompilerParams(vmem_limit_bytes=36 * 1024 * 1024),
        name="_".join(mode for segments, mode in groups) + "_layers",
    )(*[given[name][0] for name in names])


def merge_kernel(got, *rest, places):
    out_hbm, image, image_sem = rest[-3:]
    count, channels, rows, lanes = got.shape

    def image_copy(k):
        return pltpu.make_async_copy(image.at[k], out_hbm.at[:, pl.ds(16 * places[k], 16)], image_sem.at[k])

    for k in range(len(places)):
        colors = [jnp.zeros((16, lanes), f32) for channel in range(3)]
        trans = jnp.ones((16, lanes), f32)
        for source in range(count):
            value = [
                jnp.exp2(got[source, channel, 16 * k : 16 * k + 16].astype(f32) * (1.0 / STEPS) - CENTRE)
                for channel in range(4)
            ]
            colors = [old + trans * new for old, new in zip(colors, value)]
            trans = trans - trans * value[3]
        for channel in range(4):
            image[k, channel] = colors[channel] if channel < 3 else 1.0 - trans
        image_copy(k).start()
    for k in range(len(places)):
        image_copy(k).wait()


def merge(got, image, all_rows, places):
    count, channels, rows, lanes = got.shape
    whole = pl.BlockSpec(memory_space=pltpu.HBM)
    operands = [got] if image is None else [got, image]

    def kernel(*refs):
        merge_kernel(*refs, places=places)

    return pl.pallas_call(
        kernel,
        in_specs=[pl.BlockSpec(memory_space=pltpu.VMEM), whole][: len(operands)],
        out_specs=whole,
        out_shape=jax.ShapeDtypeStruct((channels, all_rows, lanes), f32),
        scratch_shapes=[
            pltpu.VMEM((len(places), channels, 16, lanes), f32),
            pltpu.SemaphoreType.DMA((len(places),)),
        ],
        input_output_aliases={} if image is None else {1: 0},
        compiler_params=pltpu.CompilerParams(vmem_limit_bytes=16 * 1024 * 1024),
        name="merge",
    )(*operands)


def local(heat, entry, table):
    count = lax.axis_size("depth")
    sides = lax.axis_size("cross")
    layers, rows, columns = heat.shape
    sight = layers * count

    def turned(value, axis, by):
        size = lax.axis_size(axis)
        return lax.ppermute(value, axis, [(i, (i + by) % size) for i in range(size)])

    before = turned(heat[-1], "depth", 1)
    after = turned(heat[0], "depth", -1)
    upper = turned(heat[:, -1, :], "cross", 1)
    lower = turned(heat[:, 0, :], "cross", -1)

    heat = pltpu.with_memory_space_constraint(heat, pltpu.HBM)
    entry = pltpu.with_memory_space_constraint(entry, pltpu.HBM)
    table = pltpu.with_memory_space_constraint(table, pltpu.HBM)
    centre, outer = ((32, 32), (64, 32)), ((0, 32), (96, 32))
    state = brick(table, heat, entry, [(centre, "mid")], sight)
    codes = brick(table, heat, entry, [(centre, "ends")], sight, before=before, after=after, upper=upper, lower=lower, state=state)
    codes, before = lax.optimization_barrier((codes, before))
    first = lax.all_to_all(codes, "depth", 0, 0, tiled=True)
    codes = brick(table, heat, entry, [(outer, "all")], sight, before=before, after=after, upper=upper, lower=lower)
    second = lax.all_to_all(codes, "depth", 0, 0, tiled=True)
    image = merge(first, None, rows, (2, 3, 4, 5))
    return merge(second, image, rows, (0, 1, 6, 7))


def solution(mesh):
    in_specs = (P("depth", "cross", None), P("depth", "cross", None), P())
    out_specs = P(None, "cross", "depth")
    return jax.shard_map(local, mesh=mesh, in_specs=in_specs, out_specs=out_specs, check_vma=False)
```

```python
import jax
import jax.numpy as jnp
import numpy as np
from jax import lax
from jax.experimental import pallas as pl
from jax.experimental.pallas import tpu as pltpu
from jax.sharding import PartitionSpec as P

LANES = 128
SUBLANES = 8
PIECE = 256
LOAD = 256
SPLIT = 32
TOGETHER = 8
f32 = jnp.float32
LANE_LOOKUP = lax.GatherDimensionNumbers(
    offset_dims=(),
    collapsed_slice_dims=(1,),
    start_index_map=(1,),
    operand_batching_dims=(0,),
    start_indices_batching_dims=(0,),
)
KAPPA = -2.0 / float(np.log(2.0))
HIGH_STEPS = 32766.0
LOW_STEPS = 65535.0
CENTRE = 16.0
STEPS = 2340.0
LEAST = 2.0**-29.9


def strip_pipeline(tables, rim_rows, inside, before_ref, after_ref, heat_hbm, entry_hbm, state_ref, out_hbm, out_ref, out_row, weights, heat, entry,
                   rows_by, first_set, second_set, heat_sem, entry_sem, out_sem, *, segments, mode, sight):
    all_rows, columns = heat_hbm.shape[1:]
    layers = heat_hbm.shape[0]
    height = segments[0][1]
    count = columns // PIECE
    strips = PIECE // LANES
    centres = {"all": list(range(1, layers + 1)), "mid": list(range(1, layers - 1)), "ends": [1, 4]}[mode]
    shift = 0 if mode == "mid" else 1
    stride = centres[1] - centres[0]
    parts = strips if height > SPLIT else 1
    share = len(centres) // parts
    batch = min(share, 128 // height)
    while share % batch or (stride > 1 and batch > 1):
        batch -= 1

    load = LOAD
    loads, each = columns // load, load // PIECE
    ahead = 2 if each == 1 else 1
    adjacent = segments[1][0] == segments[0][0] + height
    blocks_of_rows = [(segments[0][0], 0, 2 * height)] if adjacent else [(row, k * height, height) for k, (row, _) in enumerate(segments)]

    def heat_copies(p):
        cols = pl.ds(pl.multiple_of(p * load, load), load)
        into = pl.ds(pl.multiple_of(2 * LANES + p * load, LANES), load)
        found = []
        for k, (row, _) in enumerate(segments):
            low, high = max(row - 16, 0), min(row + height + 16, all_rows)
            target = pl.ds(16 - (row - low), high - low)
            pairs = [(0, 0, 2), (layers - 2, 2, 2)] if mode == "ends" else [(0, 0, layers)]
            for n, (source, first, size) in enumerate(pairs):
                found.append(
                    pltpu.make_async_copy(
                        heat_hbm.at[pl.ds(source, size), pl.ds(low, high - low), cols],
                        heat.at[k, pl.ds(first, size), target, into],
                        heat_sem.at[2 * k + n, p],
                    )
                )
        return found

    def entry_copies(p):
        cols = pl.ds(pl.multiple_of(p * load, load), load)
        found = []
        for k, (row, own, size) in enumerate(blocks_of_rows):
            if mode == "ends":
                pairs = [(0, 0, 1), (layers - 1, 1, 1)]
            else:
                pairs = [(1 if mode == "mid" else 0, 0, len(centres))]
            for n, (source, first, deep) in enumerate(pairs):
                found.append(
                    pltpu.make_async_copy(
                        entry_hbm.at[pl.ds(source, deep), pl.ds(row, size), cols],
                        entry.at[pl.ds(first, deep), pl.ds(own, size), cols],
                        entry_sem.at[2 * k + n, p],
                    )
                )
        return found

    def out_copy(p):
        here = pl.ds(p * (load // LANES), load // LANES)
        rows = pl.ds(out_row, 2 * height)
        return pltpu.make_async_copy(out_ref.at[here, :, rows], out_hbm.at[here, :, rows], out_sem.at[p])

    def start(copies):
        for copy in copies:
            copy.start()

    def wait(copies):
        for copy in copies:
            copy.wait()

    def begin():
        for p in range(min(ahead, loads)):
            start(heat_copies(p))
        for p in range(loads):
            start(entry_copies(p))
            if p + ahead < loads:
                start(heat_copies(p + ahead))
        margin = jnp.zeros(heat.shape[:2] + (height, LANES), jnp.bfloat16)
        heat[:, :, 16 : 16 + height, LANES : 2 * LANES] = margin
        heat[:, :, 16 : 16 + height, 2 * LANES + columns :] = margin
        k = lax.broadcasted_iota(jnp.int32, rows_by.shape, 1) - lax.broadcasted_iota(jnp.int32, rows_by.shape, 0)
        rows_by[...] = jnp.where(k == 17, 1.0, jnp.where(k == 15, -1.0, 0.0)).astype(jnp.bfloat16)
        across = slice(2 * LANES, 2 * LANES + columns)
        for seg, (row, _) in enumerate(segments):
            for side, at_edge, first in ((0, row == 0, 0), (1, row + height == all_rows, 16 + height)):
                if at_edge:
                    for z in range(layers):
                        rim = jnp.broadcast_to(rim_rows[side, z : z + 1, :], (16, columns))
                        heat[seg, z, first : first + 16, across] = rim.astype(jnp.bfloat16)

    def prepare(p, seg, kept, n):
        cols = pl.ds(pl.multiple_of(2 * LANES + p * PIECE, LANES), PIECE)
        wide = pl.ds(pl.multiple_of(LANES + p * PIECE, LANES), PIECE + 2 * LANES)
        mid = slice(16, 16 + height)
        for first in range(0, share, batch):
            at = n * share + first
            own = centres[0] - shift + stride * at
            window = heat[seg, pl.ds(own, batch), mid, wide].reshape(batch * height, PIECE + 2 * LANES)
            moved = jnp.dot(window, weights[...], preferred_element_type=f32).reshape(batch, height, PIECE)
            for q in range(strips):
                kept[1][q, pl.ds(at, batch)] = moved[:, :, q * LANES : (q + 1) * LANES]
            yield
            for m in range(batch):
                moved = jnp.dot(rows_by[...], heat[seg, own + m, :, cols], preferred_element_type=f32)
                for q in range(strips):
                    kept[0][q, at + m] = moved[:, q * LANES : (q + 1) * LANES]
                yield

    def looked(index):
        rg, ba = [
            lax.gather(table, index[:, :, None], LANE_LOOKUP, (1, 1), mode=lax.GatherScatterMode.PROMISE_IN_BOUNDS)
            for table in tables
        ]
        return rg.astype(f32), (rg & 0xFFFF).astype(f32), ba.astype(f32), (ba & 0xFFFF).astype(f32) * (4.0 / (sight * LOW_STEPS))

    scale = 0.7 / 9.0
    scales = [scale / (HIGH_STEPS * 65536.0), scale / LOW_STEPS, scale / (HIGH_STEPS * 65536.0)]

    def composite(p, seg, kept, qs):
        jobs = [(q, r0) for q in qs for r0 in range(0, height, SUBLANES)]
        size = min(TOGETHER, len(jobs))
        for group in range(0, len(jobs), size):
            units = []
            for q, r0 in jobs[group : group + size]:
                s = strips * p + q
                units.append(
                    dict(
                        q=q,
                        s=s,
                        r0=r0,
                        cols=pl.ds(pl.multiple_of(s * LANES, LANES), LANES),
                        trans=jnp.ones((SUBLANES, LANES), f32),
                        colors=[jnp.zeros((SUBLANES, LANES), f32) for channel in range(3)],
                    )
                )
            def layer(slot, unit):
                r0 = unit["r0"]
                rows = pl.ds(segments[seg][0] + r0, 16)
                if slot == 0 and shift:
                    return before_ref[rows, unit["cols"]].astype(f32) * inside[0]
                if slot == centres[-1] + 1 and shift:
                    return after_ref[rows, unit["cols"]].astype(f32) * inside[1]
                lanes = pl.ds(pl.multiple_of((unit["s"] + 2) * LANES, LANES), LANES)
                return heat[seg, slot - shift, 16 + r0 : 32 + r0, lanes].astype(f32)

            for at, slot in enumerate(centres):
                for number, unit in enumerate(units):
                    q, r0 = unit["q"], unit["r0"]
                    if number % 2 == 0:
                        if at == 0 or stride > 1:
                            prev, cur = layer(slot - 1, unit), layer(slot, unit)
                        else:
                            prev, cur = unit["layers"]
                        nxt = layer(slot + 1, unit)
                        unit["layers"] = cur, nxt
                        steps = nxt - prev
                    half = slice(0, 8) if number % 2 == 0 else slice(8, 16)
                    if mode == "ends" and at == 1:
                        old = [state_ref[unit["s"], channel, seg * height + r0 : seg * height + r0 + 8, :] for channel in range(4)]
                        unit["colors"] = [held + unit["trans"] * new for held, new in zip(unit["colors"], old)]
                        unit["trans"] = unit["trans"] * old[3]
                    a = steps[half]
                    b, c = [values[q, at, r0 : r0 + 8, :] for values in kept]
                    m = b + c
                    lit = a + m + m
                    square = (a * a + b * b) + (c * c + 4.0)
                    shade = lit * lit * pl.reciprocal(square, approx=True) + 0.3 / scale
                    red, green, blue, weight = looked(entry[at, seg * height + r0 : seg * height + r0 + 8, unit["cols"]])
                    alpha = weight * pl.reciprocal(jnp.exp2(cur[half] * KAPPA) + 1.0, approx=True)
                    part = alpha * unit["trans"]
                    unit["trans"] = unit["trans"] - part
                    shown = shade * part
                    unit["colors"] = [old + new * shown for old, new in zip(unit["colors"], (red, green, blue))]
                yield
            for pair in range(0, len(units), 2):
                twin = units[pair : pair + 2]
                r0 = out_row + seg * height + twin[0]["r0"]
                for channel in range(4):
                    if mode == "mid":
                        values = [unit["colors"][channel] if channel < 3 else unit["trans"] for unit in twin]
                        out_ref[twin[0]["s"], channel, r0 : r0 + 16, :] = jnp.concatenate(values, axis=0)
                        continue
                    values = [unit["colors"][channel] * scales[channel] if channel < 3 else 1.0 - unit["trans"] for unit in twin]
                    code = jnp.round((jnp.log2(jnp.maximum(jnp.concatenate(values, axis=0), LEAST)) + CENTRE) * STEPS)
                    out_ref[twin[0]["s"], channel, r0 : r0 + 16, :] = code.astype(jnp.int32).astype(jnp.int16)

    def both(first, second):
        def part(n, carry):
            qs = [n] if parts > 1 else list(range(strips))
            following = prepare(*second, n)
            groups = max(len(qs) * height // (SUBLANES * TOGETHER), 1)
            steps = max(groups * len(centres) // (share // batch * (batch + 1)), 1)
            for at, step in enumerate(composite(*first, qs)):
                if at % steps == 0:
                    next(following, None)
            for step in following:
                pass
            return carry

        if parts > 1:
            lax.fori_loop(0, parts, part, 0)
        else:
            part(0, 0)

    def run():
        for p in range(min(ahead, loads)):
            wait(heat_copies(p))
        for n in range(parts):
            for step in prepare(0, 0, first_set, n):
                pass

        def body(i, carry):
            @pl.when(i % each == 0)
            def _():
                wait(entry_copies(i // each))

            @pl.when((i % each == 0) & (i // each + ahead < loads))
            def _():
                wait(heat_copies(i // each + ahead))

            both((i, 0, first_set), (i, 1, second_set))
            both((i, 1, second_set), (jnp.minimum(i + 1, count - 1), 0, first_set))

            if out_hbm is not None:

                @pl.when(i % each == each - 1)
                def _():
                    out_copy(i // each).start()

            return carry

        lax.fori_loop(0, count, body, 0)

    def finish():
        for p in range(loads if out_hbm is not None else 0):
            out_copy(p).wait()

    return begin, run, finish


def lookup_words(table_ref, padded):
    padded[...] = jnp.zeros(padded.shape, f32)
    padded[0:4, 0 : table_ref.shape[1]] = table_ref[...]
    tables = []
    for pair in range(2):
        low_half = jnp.round(padded[2 * pair + 1 : 2 * pair + 2, :] * LOW_STEPS)
        high_half = jnp.round(padded[2 * pair : 2 * pair + 1, :] * HIGH_STEPS - low_half * (1.0 / 65536.0))
        words = high_half.astype(jnp.int32) * 65536 + low_half.astype(jnp.int32)
        tables.append(jnp.broadcast_to(words, (SUBLANES, LANES)))
    return tables


def brick(table, heat, entry, groups, sight, before=None, after=None, upper=None, lower=None, state=None):
    layers, all_rows, columns = heat.shape
    pieces = columns // PIECE
    blocks = columns // LANES
    rows_of = [2 * segments[0][1] for segments, mode in groups]
    total = sum(rows_of)
    direct = groups[0][1] == "mid"
    out_type = f32 if direct else jnp.int16
    whole = pl.BlockSpec(memory_space=pltpu.HBM)
    inside = pl.BlockSpec(memory_space=pltpu.VMEM)
    given = {"table": (table, whole), "heat": (heat, whole), "entry": (entry, whole)}
    if before is not None:
        given["before"], given["after"] = (before, inside), (after, inside)
    if upper is not None:
        given["upper"], given["lower"] = (upper, inside), (lower, inside)
    if state is not None:
        given["state"] = (state, inside)
    names = list(given)
    common = [
        pltpu.VMEM(table.shape, f32),
        pltpu.VMEM((SUBLANES, LANES), f32),
        pltpu.VMEM((2, layers, columns), f32),
        pltpu.VMEM((PIECE + 2 * LANES, PIECE), jnp.bfloat16),
        pltpu.VMEM((SUBLANES, LANES) if direct else (blocks, 4, total, LANES), out_type),
        pltpu.SemaphoreType.DMA,
    ]
    own = []
    for segments, mode in groups:
        height = segments[0][1]
        held, centres = {"all": (layers, layers), "mid": (layers, layers - 2), "ends": (4, 2)}[mode]
        kept = [pltpu.VMEM((PIECE // LANES, centres, height, LANES), f32) for number in range(2)]
        own += [
            pltpu.VMEM((2, held, height + 32, columns + 3 * LANES), jnp.bfloat16),
            pltpu.VMEM((centres, 2 * height, columns), jnp.int32),
            pltpu.VMEM((height, height + 32), jnp.bfloat16),
            kept,
            kept,
            pltpu.SemaphoreType.DMA((4, pieces)),
            pltpu.SemaphoreType.DMA((4, pieces)),
            pltpu.SemaphoreType.DMA((pieces,)),
        ]

    def kernel(*refs):
        ref = dict(zip(names, refs))
        out_hbm = refs[len(names)]
        table_ref, padded, rim_rows, weights, out_ref, table_sem, *rest = refs[len(names) + 1 :]
        if direct:
            out_hbm, out_ref = None, out_hbm
        here, side = lax.axis_index("depth"), lax.axis_index("cross")
        flags = [(here > 0).astype(f32), (here < lax.axis_size("depth") - 1).astype(f32)]
        table_copy = pltpu.make_async_copy(ref["table"], table_ref, table_sem)
        table_copy.start()
        tables = []
        runs, row = [], 0
        for n, (segments, mode) in enumerate(groups):
            runs.append(
                strip_pipeline(tables, rim_rows, flags, ref.get("before"), ref.get("after"), ref["heat"], ref["entry"], ref.get("state"),
                               out_hbm, out_ref, row, weights, *rest[8 * n : 8 * n + 8], segments=segments, mode=mode, sight=sight)
            )
            row += rows_of[n]
        if upper is not None:
            rim_rows[0] = ref["upper"][...].astype(f32) * (side > 0).astype(f32)
            rim_rows[1] = ref["lower"][...].astype(f32) * (side < lax.axis_size("cross") - 1).astype(f32)
        for begin, run, finish in runs:
            begin()
        k = lax.broadcasted_iota(jnp.int32, weights.shape, 0) - lax.broadcasted_iota(jnp.int32, weights.shape, 1)
        weights[...] = jnp.where(k == LANES + 1, 1.0, jnp.where(k == LANES - 1, -1.0, 0.0)).astype(jnp.bfloat16)
        table_copy.wait()
        tables += lookup_words(table_ref, padded)
        for begin, run, finish in runs:
            run()
        for begin, run, finish in runs:
            finish()

    return pl.pallas_call(
        kernel,
        in_specs=[given[name][1] for name in names],
        out_specs=inside if direct else whole,
        out_shape=jax.ShapeDtypeStruct((blocks, 4, total, LANES), out_type),
        scratch_shapes=common + own,
        compiler_params=pltpu.CompilerParams(vmem_limit_bytes=36 * 1024 * 1024),
        name="_".join(mode for segments, mode in groups) + "_layers",
    )(*[given[name][0] for name in names])


def merge_kernel(got, *rest, places):
    out_hbm, image, image_sem = rest[-3:]
    count, channels, rows, lanes = got.shape

    def image_copy(k):
        return pltpu.make_async_copy(image.at[k], out_hbm.at[:, pl.ds(16 * places[k], 16)], image_sem.at[k])

    for k in range(len(places)):
        colors = [jnp.zeros((16, lanes), f32) for channel in range(3)]
        trans = jnp.ones((16, lanes), f32)
        for source in range(count):
            value = [
                jnp.exp2(got[source, channel, 16 * k : 16 * k + 16].astype(f32) * (1.0 / STEPS) - CENTRE)
                for channel in range(4)
            ]
            colors = [old + trans * new for old, new in zip(colors, value)]
            trans = trans - trans * value[3]
        for channel in range(4):
            image[k, channel] = colors[channel] if channel < 3 else 1.0 - trans
        image_copy(k).start()
    for k in range(len(places)):
        image_copy(k).wait()


def merge(got, image, all_rows, places):
    count, channels, rows, lanes = got.shape
    whole = pl.BlockSpec(memory_space=pltpu.HBM)
    operands = [got] if image is None else [got, image]

    def kernel(*refs):
        merge_kernel(*refs, places=places)

    return pl.pallas_call(
        kernel,
        in_specs=[pl.BlockSpec(memory_space=pltpu.VMEM), whole][: len(operands)],
        out_specs=whole,
        out_shape=jax.ShapeDtypeStruct((channels, all_rows, lanes), f32),
        scratch_shapes=[
            pltpu.VMEM((len(places), channels, 16, lanes), f32),
            pltpu.SemaphoreType.DMA((len(places),)),
        ],
        input_output_aliases={} if image is None else {1: 0},
        compiler_params=pltpu.CompilerParams(vmem_limit_bytes=16 * 1024 * 1024),
        name="merge",
    )(*operands)


def local(heat, entry, table):
    count = lax.axis_size("depth")
    sides = lax.axis_size("cross")
    layers, rows, columns = heat.shape
    sight = layers * count

    def turned(value, axis, by):
        size = lax.axis_size(axis)
        return lax.ppermute(value, axis, [(i, (i + by) % size) for i in range(size)])

    before = turned(heat[-1], "depth", 1)
    after = turned(heat[0], "depth", -1)
    upper = turned(heat[:, -1, :], "cross", 1)
    lower = turned(heat[:, 0, :], "cross", -1)

    heat = pltpu.with_memory_space_constraint(heat, pltpu.HBM)
    entry = pltpu.with_memory_space_constraint(entry, pltpu.HBM)
    table = pltpu.with_memory_space_constraint(table, pltpu.HBM)
    centre, outer = ((32, 32), (64, 32)), ((0, 32), (96, 32))
    state = brick(table, heat, entry, [(centre, "mid")], sight)
    codes = brick(table, heat, entry, [(centre, "ends")], sight, before=before, after=after, upper=upper, lower=lower, state=state)
    codes, before = lax.optimization_barrier((codes, before))
    first = lax.all_to_all(codes, "depth", 0, 0, tiled=True)
    codes = brick(table, heat, entry, [(outer, "all")], sight, before=before, after=after, upper=upper, lower=lower)
    second = lax.all_to_all(codes, "depth", 0, 0, tiled=True)
    image = merge(first, None, rows, (2, 3, 4, 5))
    return merge(second, image, rows, (0, 1, 6, 7))


def solution(mesh):
    in_specs = (P("depth", "cross", None), P("depth", "cross", None), P())
    out_specs = P(None, "cross", "depth")
    return jax.shard_map(local, mesh=mesh, in_specs=in_specs, out_specs=out_specs, check_vma=False)
```
